512 devices in a mesh: dict: 64 (over y_lo, z, core), dp: 8 (over x, y_hi).
Axes of the slice: x: 4, y: 8 (y_hi: 2, y_lo: 4; y = y_hi * 4 + y_lo), z: 8, core: 2. Of those that a mesh axis runs over, the one named last changes fastest.
Arguments:
- activations: bfloat16 [2048, 4608], P('dp', 'dict'), may hold values from -6 to 6
- enc_weight: bfloat16 [4608, 8192], P(None, 'dict'), may hold values from -0.09375 to 0.09375
- enc_bias: bfloat16 [8192], P('dict'), may hold values from -3 to 3
- dec_weight: bfloat16 [8192, 4608], P('dict'), may hold values from -0.125 to 0.125
- dec_bias: bfloat16 [4608], replicated, may hold values from -4 to 4
- thresholds: int32 [8192], P('dict'), may hold values from 4 to 16
- active_blocks: int32 [16, 32], P('dp'), may hold values from 0 to 63, all different within a row
Outputs:
- grad_enc_weight: bfloat16 [4608, 8192], P(None, 'dict')
- grad_dec_weight: bfloat16 [8192, 4608], P('dict')
- grad_enc_bias: bfloat16 [8192], P('dict')
- grad_dec_bias: bfloat16 [4608], replicated
The draws below stay inside these ranges and needn't reach their ends.
Inputs may be any that keep to these rules, and one draw needn't show every extreme that they name: `active_blocks`: each row lists 32 different blocks, and every block is listed by some row.
All inputs are finite; a program needn't handle non-finite values.
Results may differ from the reference program's by a relative error of at most 0.02.
Values may be sent and summed in bfloat16 or wider, within the bound.
No kernel may reach another device: no remote copies, remote signals or barrier semaphores. Data moves between devices by JAX's collectives and lax.ppermute only.
A program may use at most 64 MiB of HBM per device.

```python
import math
import jax
import jax.numpy as jnp
from jax import lax

D = 4608
TILE = 128
TOK_DEV = 256
TOKENS = 2048
LATENTS = 8192
TILES = 16
ACTIVE = 32
N_DICT = 64
N_DP = 8


def place_ends(values, rng, smallest, largest):
    spot = [jax.random.randint(jax.random.fold_in(rng, axis), (), 0, length) for axis, length in enumerate(values.shape)]
    longest = values.shape.index(max(values.shape))
    neighbour = spot[:longest] + [(spot[longest] + 1) % values.shape[longest]] + spot[longest + 1:]
    return values.at[tuple(spot)].set(smallest).at[tuple(neighbour)].set(largest)


def levels(stream_key, dims, split, low, top_value):
    level = 1.0
    for position, parts in split:
        steps = jax.random.uniform(jax.random.fold_in(jax.random.fold_in(stream_key, 6), position), (parts,), jnp.float32, low / len(split), top_value / len(split))
        level = level * jnp.repeat(jnp.exp(steps), dims[position] // parts).reshape((-1,) + (1,) * (len(dims) - 1 - position))
    return level


def distinct(key, rows, number_of, top, lift):
    order = jax.random.permutation(jax.random.fold_in(key, 1), number_of)
    pull = order
    for power in range(3):
        pull = pull * pull // number_of
    pull = pull * lift // number_of
    tickets = jax.random.randint(jax.random.fold_in(key, 2), (rows, number_of), 0, 4096) + pull
    holders = jax.random.permutation(jax.random.fold_in(key, 3), rows)[jnp.arange(number_of) % rows]
    tickets = jnp.where(jnp.arange(rows)[:, None] == holders[None, :], 1 << 14, tickets)
    priority = tickets * number_of + jnp.arange(number_of)
    return lax.top_k(priority.astype(jnp.int32), top)[1].astype(jnp.int32)


def scatter_about(rng, extent, deviation, bound, shards=(), held_as=jnp.bfloat16):
    factor_of = levels(rng, extent, shards, -0.22, 0.18) if shards else 1.0
    array = jax.random.normal(rng, extent, jnp.float32) * deviation * factor_of
    return jnp.minimum(jnp.maximum(array, -bound), bound).astype(held_as)


def setup_inputs(seed: int = 0) -> dict:
    streams_of = jax.random.split(jax.random.key(seed), 8)
    return {
        "activations": scatter_about(streams_of[0], (TOKENS, D), 1.0, 6.0, ((0, 8), (1, 64))),
        "enc_weight": scatter_about(streams_of[1], (D, LATENTS), D ** -0.5, 0.09375, ((1, 64),)),
        "enc_bias": scatter_about(streams_of[2], (LATENTS,), 0.5, 3.0, ((0, 64),)),
        "dec_weight": scatter_about(streams_of[3], (LATENTS, D), (ACTIVE * TILE // 2) ** -0.5, 0.125, ((0, 64),)),
        "dec_bias": scatter_about(streams_of[4], (D,), 1.0, 4.0),
        "thresholds": place_ends(jax.random.randint(streams_of[5], (LATENTS,), 4, 17), jax.random.fold_in(streams_of[5], 1), 4, 16).astype(jnp.int32),
        "active_blocks": distinct(streams_of[6], TILES, N_DICT, ACTIVE, 8192),
    }


sharpness = 4.0

def roundtrip(value):
    return lax.optimization_barrier(value.astype(jnp.bfloat16)).astype(jnp.float32)

def reference(activations, enc_weight, enc_bias, dec_weight, dec_bias, thresholds, active_blocks):
    tokens = activations.shape[0]
    latents = enc_weight.shape[1]
    blocks = latents // TILE
    block_ids = jnp.arange(blocks, dtype=jnp.int32)
    tile_on = jnp.any(active_blocks[:, :, None] == block_ids[None, None, :], axis=1).astype(jnp.float32)
    live = jnp.repeat(jnp.repeat(tile_on, TILE, axis=0), TILE, axis=1)
    pre_act = jnp.dot(activations, enc_weight, preferred_element_type=jnp.float32) + enc_bias.astype(jnp.float32)
    theta = thresholds.astype(jnp.float32) / 16.0
    gate_prob = jax.nn.sigmoid(sharpness * (pre_act - theta[None, :]))
    features = (live * pre_act * gate_prob).astype(jnp.bfloat16)
    recon = jnp.dot(features, dec_weight, preferred_element_type=jnp.float32) + dec_bias.astype(jnp.float32)
    residual = ((recon - activations.astype(jnp.float32)) / math.sqrt(tokens)).astype(jnp.bfloat16)
    dfeat = jnp.dot(residual, dec_weight.T, preferred_element_type=jnp.float32)
    dpre = dfeat * live * (gate_prob + sharpness * pre_act * gate_prob * (1.0 - gate_prob))
    dpre_b = dpre.astype(jnp.bfloat16)
    enc_total = jnp.zeros(enc_weight.shape, jnp.float32)
    dec_total = jnp.zeros(dec_weight.shape, jnp.float32)
    ebias_total = jnp.zeros((latents,), jnp.float32)
    dbias_total = jnp.zeros((activations.shape[1],), jnp.float32)
    for shard_index in range(N_DP):
        first = shard_index * TOK_DEV
        act_rows = activations[first:first + TOK_DEV]
        feat_rows = features[first:first + TOK_DEV]
        res_rows = residual[first:first + TOK_DEV]
        dpre_rows = dpre[first:first + TOK_DEV]
        dpre_brows = dpre_b[first:first + TOK_DEV]
        enc_total = enc_total + roundtrip(jnp.dot(act_rows.T, dpre_brows, preferred_element_type=jnp.float32))
        dec_total = dec_total + roundtrip(jnp.dot(feat_rows.T, res_rows, preferred_element_type=jnp.float32))
        ebias_total = ebias_total + roundtrip(lax.optimization_barrier(jnp.sum(dpre_rows, axis=0)))
        dbias_total = dbias_total + roundtrip(lax.optimization_barrier(jnp.sum(res_rows.astype(jnp.float32), axis=0)))
    return (enc_total.astype(jnp.bfloat16), dec_total.astype(jnp.bfloat16), ebias_total.astype(jnp.bfloat16), dbias_total.astype(jnp.bfloat16))
```

```python
import math

import jax
import jax.numpy as jnp
import numpy as np
from jax import lax
from jax.sharding import PartitionSpec as P

TILE = 128
SHARPNESS = 4.0
F32 = jnp.float32
BF16 = jnp.bfloat16

GRID = (2, 2, 4, 2, 2)
FAR, NEAR, CORE = (0, 2), (1, 3), (4,)


def groups(axes):
    index = np.arange(math.prod(GRID)).reshape(GRID)
    rest = [axis for axis in range(len(GRID)) if axis not in axes]
    size = math.prod(GRID[axis] for axis in axes)
    return index.transpose(rest + list(axes)).reshape(-1, size).tolist()


def exchange(parts, axes):
    return lax.all_to_all(parts, "dict", 0, 0, axis_index_groups=groups(axes))


def spread(block, axes):
    size = math.prod(GRID[axis] for axis in axes)
    return exchange(jnp.broadcast_to(block[None], (size,) + block.shape), axes)


def gather_dict(block):
    whole = spread(spread(spread(block, FAR), NEAR), CORE)
    whole = whole.reshape((2, 2, 2, 2, 4) + block.shape)
    return whole.transpose(3, 1, 4, 2, 0, 5, 6).reshape(-1, block.shape[1])


def scatter_dict(total):
    cols, rows = total.shape[0] // math.prod(GRID), total.shape[1]
    parts = total.reshape(GRID + (cols, rows)).transpose(4, 1, 3, 0, 2, 5, 6)
    for axes in (CORE, NEAR, FAR):
        size = math.prod(GRID[axis] for axis in axes)
        parts = exchange(parts.astype(BF16).reshape(size, -1, rows), axes)
        parts = jnp.sum(parts.astype(F32), axis=0)
    return parts


def sum_dp(partial, count):
    parts = lax.all_to_all(partial.reshape(count, -1, partial.shape[1]), "dp", 0, 0)
    mine = jnp.sum(parts.astype(F32), axis=0).astype(BF16)
    whole = lax.all_to_all(jnp.broadcast_to(mine[None], (count,) + mine.shape), "dp", 0, 0)
    return whole.reshape(partial.shape)


def local(activations, enc_weight, enc_bias, dec_weight, dec_bias, thresholds, active_blocks):
    n_dp = lax.axis_size("dp")
    scale_root = math.sqrt(activations.shape[0] * n_dp)
    own = activations.T
    cols = own.shape[0]
    act = gather_dict(own)
    dict_index = lax.axis_index("dict")
    tile_live = jnp.any(active_blocks == dict_index, axis=1).astype(F32)
    row_live = jnp.repeat(tile_live, TILE)[:, None]
    theta = thresholds.astype(F32) / 16.0
    pre = lax.dot_general(act, enc_weight, (((0,), (0,)), ((), ())), preferred_element_type=F32)
    pre = pre + enc_bias.astype(F32)[None, :]
    gate = jax.nn.sigmoid(SHARPNESS * (pre - theta[None, :]))
    features = (row_live * pre * gate).astype(BF16)

    partial = lax.dot_general(
        dec_weight, features, (((0,), (1,)), ((), ())), preferred_element_type=F32
    ).astype(BF16)
    bias = lax.dynamic_slice_in_dim(dec_bias, dict_index * cols, cols).astype(F32)
    recon = scatter_dict(partial) + bias[:, None]
    residual = gather_dict(((recon - own.astype(F32)) / scale_root).astype(BF16))

    dec_part = lax.dot_general(
        features, residual, (((0,), (1,)), ((), ())), preferred_element_type=F32
    ).astype(BF16)
    dfeat = lax.dot_general(
        residual, dec_weight, (((0,), (1,)), ((), ())), preferred_element_type=F32
    )
    dpre = dfeat * row_live * (gate + SHARPNESS * pre * gate * (1.0 - gate))
    enc_part = lax.dot_general(
        act, dpre.astype(BF16), (((1,), (0,)), ((), ())), preferred_element_type=F32
    ).astype(BF16)
    bias_part = jnp.concatenate(
        [jnp.sum(dpre, axis=0), jnp.sum(residual.astype(F32), axis=1)]
    ).astype(BF16)
    bias_part = bias_part.reshape(-1, TILE)
    bias_parts = lax.all_to_all(
        jnp.broadcast_to(bias_part[None], (n_dp,) + bias_part.shape), "dp", 0, 0
    )
    bias_sum = jnp.sum(bias_parts.astype(F32), axis=0).astype(BF16)
    return (
        sum_dp(enc_part, n_dp),
        sum_dp(dec_part, n_dp),
        bias_sum[0],
        bias_sum[1:].reshape(-1),
    )


def solution(mesh):
    placed = (
        P("dp", "dict"),
        P(None, "dict"),
        P("dict"),
        P("dict", None),
        P(),
        P("dict"),
        P("dp", None),
    )
    return jax.shard_map(
        local,
        mesh=mesh,
        in_specs=placed,
        out_specs=(P(None, "dict"), P("dict", None), P("dict"), P()),
        check_vma=False,
    )
```

```python
import math

import jax
import jax.numpy as jnp
import numpy as np
from jax import lax
from jax.experimental import pallas as pl
from jax.experimental.pallas import tpu as pltpu
from jax.sharding import PartitionSpec as P

TILE = 128
SHARPNESS = 4.0
F32 = jnp.float32
BF16 = jnp.bfloat16

GRID = (2, 2, 4, 2, 2)
FAR, NEAR, CORE = (0, 2), (1, 3), (4,)
CHIPS = 32
NX = 4
BIAS_ROWS = 48
VMEM = 48 * 1024 * 1024


def size_of(axes):
    return math.prod(GRID[axis] for axis in axes)


def groups(axes):
    index = np.arange(math.prod(GRID)).reshape(GRID)
    rest = [axis for axis in range(len(GRID)) if axis not in axes]
    return index.transpose(rest + list(axes)).reshape(-1, size_of(axes)).tolist()


X_GROUPS = np.arange(8).reshape(NX, 2).T.tolist()
CORE_SWAP = [(i, i ^ 1) for i in range(64)]
Y_SWAP = [(i, i ^ 1) for i in range(8)]


def exchange(parts, axes):
    return lax.all_to_all(parts, "dict", 0, 0, axis_index_groups=groups(axes))


def spread(block, axes):
    return exchange(jnp.broadcast_to(block[None], (size_of(axes),) + block.shape), axes)


def gather_chips(block):
    return spread(spread(block, FAR), NEAR)


def chip_blocks():
    for near in range(4):
        for far in range(8):
            y, z = (far // 4) * 2 + near // 2, (far % 4) * 2 + near % 2
            yield near, far, y * 8 + z


def in_order(parts_ref, whole_ref):
    cols = parts_ref.shape[2]
    for near, far, chip in chip_blocks():
        whole_ref[chip * cols : (chip + 1) * cols, :] = parts_ref[near, far]


def dot(a, b, dims):
    return lax.dot_general(a, b, (dims, ((), ())), preferred_element_type=F32)


def forward_kernel(
    act_ref, we_own, we_other, wd_own, wd_other, row_ref, parts_ref, feat_ref, slope_ref, act
):
    in_order(act_ref, act)
    for n, we in enumerate((we_own, we_other)):
        lanes = slice(n * TILE, (n + 1) * TILE)
        bias, theta, live = row_ref[0:1, lanes], row_ref[1:2, lanes], row_ref[2:3, lanes]
        pre = dot(act[...], we[...], ((0,), (0,))) + bias
        gate = jax.nn.sigmoid(SHARPNESS * (pre - theta))
        feat_ref[:, lanes] = (live * pre * gate).astype(BF16)
        slope_ref[:, lanes] = live * (gate + SHARPNESS * pre * gate * (1.0 - gate))
    cols = parts_ref.shape[2]
    step = 8 * cols
    place = {chip: (near, far) for near, far, chip in chip_blocks()}
    for first in range(0, act.shape[0], step):
        span = slice(first, first + step)
        total = dot(feat_ref[:, :TILE], wd_own[:, span], ((1,), (0,)))
        total = total + dot(feat_ref[:, TILE:], wd_other[:, span], ((1,), (0,)))
        turned = total.astype(BF16).T
        for i in range(8):
            near, far = place[first // cols + i]
            parts_ref[near, far] = turned[i * cols : (i + 1) * cols, :]


def backward_kernel(
    res_ref, act_ref, wd_own, wd_other, feat_ref, slope_ref, own_ref, other_ref, act, res, bias
):
    in_order(act_ref, act)
    in_order(res_ref, res)
    d = act.shape[0]
    quarter, lat = d // NX, TILE // NX
    res_t = res[...].T
    feat_t = jnp.concatenate([feat_ref[...].T, jnp.ones((16, TILE), BF16)], axis=0)
    bias[...] = jnp.zeros_like(bias)
    for i in range(d // TILE):
        tile = dot(feat_t, res[i * TILE : (i + 1) * TILE, :], ((1,), (1,)))
        bias[i + 1 : i + 2, :] = tile[2 * TILE : 2 * TILE + 1, :]
        tile = tile.astype(BF16)
        for x in range(NX):
            rows = slice(quarter + i * lat, quarter + (i + 1) * lat)
            own_ref[x, rows, :] = tile[x * lat : (x + 1) * lat, :]
            other_ref[x, rows, :] = tile[TILE + x * lat : TILE + (x + 1) * lat, :]
    for n, (wd, out) in enumerate(((wd_own, own_ref), (wd_other, other_ref))):
        dfeat = dot(res_t, wd[...], ((1,), (1,)))
        dpre = dfeat * slope_ref[:, n * TILE : (n + 1) * TILE]
        bias[0:1, :] = jnp.sum(dpre, axis=0, keepdims=True)
        dpre = dpre.astype(BF16)
        rows = bias[...].astype(BF16)
        for x in range(NX):
            enc = dot(act[x * quarter : (x + 1) * quarter, :], dpre, ((1,), (0,)))
            out[x, :quarter, :] = enc.astype(BF16)
            out[x, 2 * quarter :, :] = rows


def unpack_kernel(first_ref, second_ref, third_ref, enc_ref, dec_ref):
    quarter, lat = enc_ref.shape[0] // NX, TILE // NX
    size = first_ref.shape[1]
    rest = quarter - size
    for x in range(NX):
        enc_ref[x * quarter : x * quarter + size, :] = first_ref[x]
        enc_ref[x * quarter + size : (x + 1) * quarter, :] = second_ref[x, :rest, :]
        for i in range(enc_ref.shape[0] // TILE):
            at = rest + i * lat
            ref = second_ref if at < size else third_ref
            at = at % size
            dec_ref[x * lat : (x + 1) * lat, i * TILE : (i + 1) * TILE] = ref[x, at : at + lat, :]


def call(kernel, outs, args, scratch=(), flops=0):
    whole = pl.BlockSpec(memory_space=pltpu.VMEM)
    moved = sum(a.size * a.dtype.itemsize for a in args)
    moved += sum(math.prod(s.shape) * s.dtype.itemsize for s in outs)
    return pl.pallas_call(
        kernel,
        out_shape=outs,
        in_specs=[whole] * len(args),
        out_specs=[whole] * len(outs),
        scratch_shapes=list(scratch),
        compiler_params=pltpu.CompilerParams(vmem_limit_bytes=VMEM),
        cost_estimate=pl.CostEstimate(flops=flops, bytes_accessed=moved, transcendentals=0),
    )(*args)


def shape(dims, dtype=BF16):
    return jax.ShapeDtypeStruct(dims, dtype)


def local(activations, enc_weight, enc_bias, dec_weight, dec_bias, thresholds, active_blocks):
    n_dp = lax.axis_size("dp")
    d = enc_weight.shape[0]
    scale_root = math.sqrt(activations.shape[0] * n_dp)
    dict_index = lax.axis_index("dict")
    core = dict_index % 2

    turned = activations.T
    halves = jnp.stack([turned[:, :TILE], turned[:, TILE:]])
    own = exchange(halves, CORE).reshape(-1, TILE)
    cols = own.shape[0]
    act = gather_chips(own)

    enc_other = lax.ppermute(enc_weight, "dict", CORE_SWAP)
    dec_other = lax.ppermute(dec_weight, "dict", CORE_SWAP)
    rows = jnp.stack([enc_bias.astype(F32), thresholds.astype(F32) / 16.0])
    rows = jnp.concatenate([rows, lax.ppermute(rows, "dict", CORE_SWAP)], axis=1)
    listed = lax.dynamic_slice_in_dim(active_blocks, core, 1)
    live = jnp.stack([jnp.any(listed == dict_index), jnp.any(listed == (dict_index ^ 1))])
    live = jnp.repeat(live.astype(F32), TILE)[None, :]
    rows = jnp.concatenate([rows, live, jnp.zeros((5, 2 * TILE), F32)], axis=0)

    work = 2 * d * 2 * TILE * TILE
    parts, feat, slope = call(
        forward_kernel,
        [shape(act.shape), shape((TILE, 2 * TILE)), shape((TILE, 2 * TILE), F32)],
        (act, enc_weight, enc_other, dec_weight, dec_other, rows),
        [pltpu.VMEM((d, TILE), BF16)],
        2 * work,
    )

    near_sum = jnp.sum(exchange(parts, NEAR).astype(F32), axis=0).astype(BF16)
    recon = jnp.sum(exchange(near_sum, FAR).astype(F32), axis=0)
    bias = lax.dynamic_slice_in_dim(dec_bias, dict_index // 2 * cols, cols).astype(F32)
    residual = (recon + bias[:, None] - own.astype(F32)) / scale_root
    res = gather_chips(residual.astype(BF16))

    packed = shape((NX, 2 * d // NX + BIAS_ROWS, TILE))
    mine, other = call(
        backward_kernel,
        [packed, packed],
        (res, act, dec_weight, dec_other, feat, slope),
        [
            pltpu.VMEM((d, TILE), BF16),
            pltpu.VMEM((d, TILE), BF16),
            pltpu.VMEM((BIAS_ROWS, TILE), F32),
        ],
        3 * work,
    )
    other = lax.ppermute(other, "dict", CORE_SWAP)
    mine = (mine.astype(F32) + other.astype(F32)).astype(BF16)

    parts = lax.all_to_all(mine, "dp", 0, 0, axis_index_groups=X_GROUPS)
    quarter = jnp.sum(parts.astype(F32), axis=0).astype(BF16)
    size = 2 * d // NX // 3
    bounds = [0, size, 2 * size, 3 * size + BIAS_ROWS]
    pieces = [lax.optimization_barrier(quarter[a:b]) for a, b in zip(bounds, bounds[1:])]
    swapped = [lax.ppermute(piece, "dp", Y_SWAP) for piece in pieces]
    pieces = [
        (a.astype(F32) + b.astype(F32)).astype(BF16) for a, b in zip(pieces, swapped)
    ]
    whole = [
        lax.all_gather(piece[:size], "dp", axis=0, axis_index_groups=X_GROUPS)
        for piece in pieces
    ]
    enc, dec = call(unpack_kernel, [shape((d, TILE)), shape((TILE, d))], whole)
    tail = pieces[2][size:]
    return enc, dec, tail[0], tail[1 : 1 + d // TILE].reshape(-1)


def solution(mesh):
    placed = (
        P("dp", "dict"),
        P(None, "dict"),
        P("dict"),
        P("dict", None),
        P(),
        P("dict"),
        P("dp", None),
    )
    return jax.shard_map(
        local,
        mesh=mesh,
        in_specs=placed,
        out_specs=(P(None, "dict"), P("dict", None), P("dict"), P()),
        check_vma=False,
    )
```

```python
import math

import jax
import jax.numpy as jnp
import numpy as np
from jax import lax
from jax.experimental import pallas as pl
from jax.experimental.pallas import tpu as pltpu
from jax.sharding import PartitionSpec as P

TILE = 128
SHARPNESS = 4.0
F32 = jnp.float32
BF16 = jnp.bfloat16

GRID = (2, 2, 4, 2, 2)
FAR, NEAR, CORE = (0, 2), (1, 3), (4,)
CHIPS = 32
NX = 4
DEC_BIAS_ROWS, ENC_BIAS_ROWS = 48, 16
VMEM = 48 * 1024 * 1024


def size_of(axes):
    return math.prod(GRID[axis] for axis in axes)


def groups(axes):
    index = np.arange(math.prod(GRID)).reshape(GRID)
    rest = [axis for axis in range(len(GRID)) if axis not in axes]
    return index.transpose(rest + list(axes)).reshape(-1, size_of(axes)).tolist()


X_GROUPS = np.arange(8).reshape(NX, 2).T.tolist()
CORE_SWAP = [(i, i ^ 1) for i in range(64)]
Y_SWAP = [(i, i ^ 1) for i in range(8)]


def exchange(parts, axes):
    return lax.all_to_all(parts, "dict", 0, 0, axis_index_groups=groups(axes))


def gather_near(blocks):
    half = blocks.shape[0] // 2
    return [
        lax.all_gather(part, "dict", axis=0, axis_index_groups=groups(NEAR))
        for part in (blocks[:half], blocks[half:])
    ]


def chip_blocks():
    for near in range(4):
        for far in range(8):
            y, z = (far // 4) * 2 + near // 2, (far % 4) * 2 + near % 2
            yield near, far, y * 8 + z


def in_order(first_ref, second_ref, whole_ref):
    half, cols = first_ref.shape[1:3]
    for near, far, chip in chip_blocks():
        ref = first_ref if far < half else second_ref
        whole_ref[chip * cols : (chip + 1) * cols, :] = ref[near, far % half]


def dot(a, b, dims):
    return lax.dot_general(a, b, (dims, ((), ())), preferred_element_type=F32)


def forward_kernel(
    act_0, act_1, we_own, we_other, wd_own, wd_other, row_ref, parts_ref, feat_ref, slope_ref, act
):
    in_order(act_0, act_1, act)
    for n, we in enumerate((we_own, we_other)):
        lanes = slice(n * TILE, (n + 1) * TILE)
        bias, theta, live = row_ref[0:1, lanes], row_ref[1:2, lanes], row_ref[2:3, lanes]
        pre = dot(act[...], we[...], ((0,), (0,))) + bias
        gate = jax.nn.sigmoid(SHARPNESS * (pre - theta))
        feat_ref[:, lanes] = (live * pre * gate).astype(BF16)
        slope_ref[:, lanes] = live * (gate + SHARPNESS * pre * gate * (1.0 - gate))
    cols = parts_ref.shape[2]
    step = 8 * cols
    place = {chip: (near, far) for near, far, chip in chip_blocks()}
    for first in range(0, act.shape[0], step):
        span = slice(first, first + step)
        total = dot(feat_ref[:, :TILE], wd_own[:, span], ((1,), (0,)))
        total = total + dot(feat_ref[:, TILE:], wd_other[:, span], ((1,), (0,)))
        turned = total.astype(BF16).T
        for i in range(8):
            near, far = place[first // cols + i]
            parts_ref[near, far] = turned[i * cols : (i + 1) * cols, :]


def decoder_kernel(res_0, res_1, feat_ref, own_ref, other_ref, res, bias):
    in_order(res_0, res_1, res)
    d = res.shape[0]
    quarter, lat = d // NX, TILE // NX
    feat_t = jnp.concatenate([feat_ref[...].T, jnp.ones((16, TILE), BF16)], axis=0)
    bias[...] = jnp.zeros_like(bias)
    for i in range(d // TILE):
        tile = dot(feat_t, res[i * TILE : (i + 1) * TILE, :], ((1,), (1,)))
        bias[i : i + 1, :] = tile[2 * TILE : 2 * TILE + 1, :]
        tile = tile.astype(BF16)
        rows = slice(i * lat, (i + 1) * lat)
        for x in range(NX):
            own_ref[x, rows, :] = tile[x * lat : (x + 1) * lat, :]
            other_ref[x, rows, :] = tile[TILE + x * lat : TILE + (x + 1) * lat, :]
    rows = bias[...].astype(BF16)
    for x in range(NX):
        own_ref[x, quarter:, :] = rows
        other_ref[x, quarter:, :] = rows


def encoder_kernel(
    res_0, res_1, act_0, act_1, wd_own, wd_other, slope_ref, own_ref, other_ref, act, res
):
    in_order(act_0, act_1, act)
    in_order(res_0, res_1, res)
    quarter = act.shape[0] // NX
    res_t = res[...].T
    for n, (wd, out) in enumerate(((wd_own, own_ref), (wd_other, other_ref))):
        dfeat = dot(res_t, wd[...], ((1,), (1,)))
        dpre = dfeat * slope_ref[:, n * TILE : (n + 1) * TILE]
        row = jnp.sum(dpre, axis=0, keepdims=True)
        rows = jnp.broadcast_to(row, (ENC_BIAS_ROWS, TILE)).astype(BF16)
        dpre = dpre.astype(BF16)
        for x in range(NX):
            enc = dot(act[x * quarter : (x + 1) * quarter, :], dpre, ((1,), (0,)))
            out[x, :quarter, :] = enc.astype(BF16)
            out[x, quarter:, :] = rows


def unpack_kernel(first_ref, second_ref, third_ref, enc_ref, dec_ref):
    quarter, lat = enc_ref.shape[0] // NX, TILE // NX
    size = first_ref.shape[1]
    rest = quarter - size
    for x in range(NX):
        enc_ref[x * quarter : x * quarter + size - rest, :] = second_ref[x, rest:, :]
        enc_ref[x * quarter + size - rest : (x + 1) * quarter, :] = third_ref[x]
        for i in range(enc_ref.shape[0] // TILE):
            ref, at = (first_ref, i * lat) if i * lat < size else (second_ref, i * lat - size)
            dec_ref[x * lat : (x + 1) * lat, i * TILE : (i + 1) * TILE] = ref[x, at : at + lat, :]


def call(kernel, outs, args, scratch=(), flops=0):
    whole = pl.BlockSpec(memory_space=pltpu.VMEM)
    moved = sum(a.size * a.dtype.itemsize for a in args)
    moved += sum(math.prod(s.shape) * s.dtype.itemsize for s in outs)
    return pl.pallas_call(
        kernel,
        out_shape=outs,
        in_specs=[whole] * len(args),
        out_specs=[whole] * len(outs),
        scratch_shapes=list(scratch),
        compiler_params=pltpu.CompilerParams(vmem_limit_bytes=VMEM),
        cost_estimate=pl.CostEstimate(flops=flops, bytes_accessed=moved, transcendentals=0),
    )(*args)


def shape(dims, dtype=BF16):
    return jax.ShapeDtypeStruct(dims, dtype)


def sum_cores(own_part, other_part):
    other_part = lax.ppermute(other_part, "dict", CORE_SWAP)
    return (own_part.astype(F32) + other_part.astype(F32)).astype(BF16)


def sum_dp(total):
    parts = lax.all_to_all(total, "dp", 0, 0, axis_index_groups=X_GROUPS)
    piece = lax.optimization_barrier(jnp.sum(parts.astype(F32), axis=0).astype(BF16))
    swapped = lax.ppermute(piece, "dp", Y_SWAP)
    return (piece.astype(F32) + swapped.astype(F32)).astype(BF16)


def local(activations, enc_weight, enc_bias, dec_weight, dec_bias, thresholds, active_blocks):
    n_dp = lax.axis_size("dp")
    d = enc_weight.shape[0]
    scale_root = math.sqrt(activations.shape[0] * n_dp)
    dict_index = lax.axis_index("dict")
    core = dict_index % 2

    turned = activations.T
    halves = jnp.stack([turned[:, :TILE], turned[:, TILE:]])
    far = size_of(FAR)
    halves = jnp.broadcast_to(halves[None], (far,) + halves.shape).reshape((-1,) + halves.shape[1:])
    act = exchange(halves, FAR + CORE).reshape(far, -1, TILE)
    chip = dict_index // 2
    own = lax.dynamic_index_in_dim(act, chip // 16 * 4 + chip % 8 // 2, keepdims=False)
    cols = own.shape[0]
    act = gather_near(act)

    enc_other = lax.ppermute(enc_weight, "dict", CORE_SWAP)
    dec_other = lax.ppermute(dec_weight, "dict", CORE_SWAP)
    rows = jnp.stack([enc_bias.astype(F32), thresholds.astype(F32) / 16.0])
    rows = jnp.concatenate([rows, lax.ppermute(rows, "dict", CORE_SWAP)], axis=1)
    listed = lax.dynamic_slice_in_dim(active_blocks, core, 1)
    live = jnp.stack([jnp.any(listed == dict_index), jnp.any(listed == (dict_index ^ 1))])
    live = jnp.repeat(live.astype(F32), TILE)[None, :]
    rows = jnp.concatenate([rows, live, jnp.zeros((5, 2 * TILE), F32)], axis=0)

    work = 2 * d * 2 * TILE * TILE
    parts, feat, slope = call(
        forward_kernel,
        [
            shape((size_of(NEAR), far, cols, TILE)),
            shape((TILE, 2 * TILE)),
            shape((TILE, 2 * TILE), F32),
        ],
        (*act, enc_weight, enc_other, dec_weight, dec_other, rows),
        [pltpu.VMEM((d, TILE), BF16)],
        2 * work,
    )

    near_sum = jnp.sum(exchange(parts, NEAR).astype(F32), axis=0).astype(BF16)
    recon = jnp.sum(exchange(near_sum, FAR).astype(F32), axis=0)
    bias = lax.dynamic_slice_in_dim(dec_bias, dict_index // 2 * cols, cols).astype(F32)
    residual = (recon + bias[:, None] - own.astype(F32)) / scale_root
    residual = residual.astype(BF16)
    residual = jnp.broadcast_to(residual[None], (far,) + residual.shape)
    res = gather_near(exchange(residual, FAR))

    quarter = d // NX
    packed = shape((NX, quarter + DEC_BIAS_ROWS, TILE))
    room = pltpu.VMEM((d, TILE), BF16)
    dec_parts = call(
        decoder_kernel,
        [packed, packed],
        (*res, feat),
        [room, pltpu.VMEM((DEC_BIAS_ROWS, TILE), F32)],
        work,
    )
    dec_total = sum_cores(*dec_parts)
    dec_total, res = lax.optimization_barrier((dec_total, res))
    packed = shape((NX, quarter + ENC_BIAS_ROWS, TILE))
    enc_parts = call(
        encoder_kernel,
        [packed, packed],
        (*res, *act, dec_weight, dec_other, slope),
        [room, room],
        2 * work,
    )

    dec_piece, enc_piece = sum_dp(dec_total), sum_dp(sum_cores(*enc_parts))
    size = 2 * quarter // 3
    pieces = (
        dec_piece[:size],
        jnp.concatenate([dec_piece[size:quarter], enc_piece[: 2 * size - quarter]]),
        enc_piece[2 * size - quarter : quarter],
    )
    whole = [
        lax.all_gather(piece, "dp", axis=0, axis_index_groups=X_GROUPS) for piece in pieces
    ]
    enc, dec = call(unpack_kernel, [shape((d, TILE)), shape((TILE, d))], whole)
    dec_bias_sum = dec_piece[quarter : quarter + d // TILE].reshape(-1)
    return enc, dec, enc_piece[quarter], dec_bias_sum


def solution(mesh):
    placed = (
        P("dp", "dict"),
        P(None, "dict"),
        P("dict"),
        P("dict", None),
        P(),
        P("dict"),
        P("dp", None),
    )
    return jax.shard_map(
        local,
        mesh=mesh,
        in_specs=placed,
        out_specs=(P(None, "dict"), P("dict", None), P("dict"), P()),
        check_vma=False,
    )
```

```python
import math

import jax
import jax.numpy as jnp
import numpy as np
from jax import lax
from jax.experimental import pallas as pl
from jax.experimental.pallas import tpu as pltpu
from jax.sharding import PartitionSpec as P

TILE = 128
SHARPNESS = 4.0
F32 = jnp.float32
BF16 = jnp.bfloat16

GRID = (2, 2, 4, 2, 2)
FAR, NEAR, CORE = (0, 2), (1, 3), (4,)
CHIPS = 32
NX = 4
DEC_BIAS_ROWS, ENC_BIAS_ROWS = 48, 16
VMEM = 48 * 1024 * 1024


def size_of(axes):
    return math.prod(GRID[axis] for axis in axes)


def groups(axes):
    index = np.arange(math.prod(GRID)).reshape(GRID)
    rest = [axis for axis in range(len(GRID)) if axis not in axes]
    return index.transpose(rest + list(axes)).reshape(-1, size_of(axes)).tolist()


X_GROUPS = np.arange(8).reshape(NX, 2).T.tolist()
CORE_SWAP = [(i, i ^ 1) for i in range(64)]
Y_SWAP = [(i, i ^ 1) for i in range(8)]


def exchange(parts, axes):
    return lax.all_to_all(parts, "dict", 0, 0, axis_index_groups=groups(axes))


def spread(block, axes):
    return exchange(jnp.broadcast_to(block[None], (size_of(axes),) + block.shape), axes)


def chip_blocks():
    for near in range(4):
        for far in range(8):
            y, z = (far // 4) * 2 + near // 2, (far % 4) * 2 + near % 2
            yield near, far, y * 8 + z


def in_order(parts_ref, whole_ref):
    cols = parts_ref.shape[2]
    for near, far, chip in chip_blocks():
        whole_ref[chip * cols : (chip + 1) * cols, :] = parts_ref[near, far]


def dot(a, b, dims):
    return lax.dot_general(a, b, (dims, ((), ())), preferred_element_type=F32)


def forward_kernel(
    act_ref, we_own, we_other, wd_own, wd_other, row_ref, parts_ref, feat_ref, slope_ref, act
):
    in_order(act_ref, act)
    for n, we in enumerate((we_own, we_other)):
        lanes = slice(n * TILE, (n + 1) * TILE)
        bias, theta, live = row_ref[0:1, lanes], row_ref[1:2, lanes], row_ref[2:3, lanes]
        pre = dot(act[...], we[...], ((0,), (0,))) + bias
        gate = jax.nn.sigmoid(SHARPNESS * (pre - theta))
        feat_ref[:, lanes] = (live * pre * gate).astype(BF16)
        slope_ref[:, lanes] = live * (gate + SHARPNESS * pre * gate * (1.0 - gate))
    cols = parts_ref.shape[2]
    step = 8 * cols
    place = {chip: (near, far) for near, far, chip in chip_blocks()}
    for first in range(0, act.shape[0], step):
        span = slice(first, first + step)
        total = dot(feat_ref[:, :TILE], wd_own[:, span], ((1,), (0,)))
        total = total + dot(feat_ref[:, TILE:], wd_other[:, span], ((1,), (0,)))
        turned = total.astype(BF16).T
        for i in range(8):
            near, far = place[first // cols + i]
            parts_ref[near, far] = turned[i * cols : (i + 1) * cols, :]


def decoder_kernel(res_ref, feat_ref, own_ref, other_ref, res, bias):
    in_order(res_ref, res)
    d = res.shape[0]
    quarter, lat = d // NX, TILE // NX
    feat_t = jnp.concatenate([feat_ref[...].T, jnp.ones((16, TILE), BF16)], axis=0)
    bias[...] = jnp.zeros_like(bias)
    for i in range(d // TILE):
        tile = dot(feat_t, res[i * TILE : (i + 1) * TILE, :], ((1,), (1,)))
        bias[i : i + 1, :] = tile[2 * TILE : 2 * TILE + 1, :]
        tile = tile.astype(BF16)
        rows = slice(i * lat, (i + 1) * lat)
        for x in range(NX):
            own_ref[x, rows, :] = tile[x * lat : (x + 1) * lat, :]
            other_ref[x, rows, :] = tile[TILE + x * lat : TILE + (x + 1) * lat, :]
    rows = bias[...].astype(BF16)
    for x in range(NX):
        own_ref[x, quarter:, :] = rows
        other_ref[x, quarter:, :] = rows


def encoder_kernel(
    res_ref, act_ref, wd_own, wd_other, slope_ref, own_ref, other_ref, act, res
):
    in_order(act_ref, act)
    in_order(res_ref, res)
    quarter = act.shape[0] // NX
    res_t = res[...].T
    for n, (wd, out) in enumerate(((wd_own, own_ref), (wd_other, other_ref))):
        dfeat = dot(res_t, wd[...], ((1,), (1,)))
        dpre = dfeat * slope_ref[:, n * TILE : (n + 1) * TILE]
        row = jnp.sum(dpre, axis=0, keepdims=True)
        rows = jnp.broadcast_to(row, (ENC_BIAS_ROWS, TILE)).astype(BF16)
        dpre = dpre.astype(BF16)
        for x in range(NX):
            enc = dot(act[x * quarter : (x + 1) * quarter, :], dpre, ((1,), (0,)))
            out[x, :quarter, :] = enc.astype(BF16)
            out[x, quarter:, :] = rows


def unpack_kernel(parts_ref, dec_ref):
    lat = dec_ref.shape[0] // NX
    for x in range(NX):
        for i in range(dec_ref.shape[1] // TILE):
            rows, lanes = slice(i * lat, (i + 1) * lat), slice(i * TILE, (i + 1) * TILE)
            dec_ref[x * lat : (x + 1) * lat, lanes] = parts_ref[x, rows, :]


def call(kernel, outs, args, scratch=(), flops=0):
    whole = pl.BlockSpec(memory_space=pltpu.VMEM)
    moved = sum(a.size * a.dtype.itemsize for a in args)
    moved += sum(math.prod(s.shape) * s.dtype.itemsize for s in outs)
    return pl.pallas_call(
        kernel,
        out_shape=outs,
        in_specs=[whole] * len(args),
        out_specs=[whole] * len(outs),
        scratch_shapes=list(scratch),
        compiler_params=pltpu.CompilerParams(vmem_limit_bytes=VMEM),
        cost_estimate=pl.CostEstimate(flops=flops, bytes_accessed=moved, transcendentals=0),
    )(*args)


def shape(dims, dtype=BF16):
    return jax.ShapeDtypeStruct(dims, dtype)


def exchange_x(parts):
    return lax.all_to_all(parts, "dp", 0, 0, axis_index_groups=X_GROUPS)


def sum_parts(parts):
    return lax.optimization_barrier(jnp.sum(parts.astype(F32), axis=0).astype(BF16))


def add(a, b):
    return (a.astype(F32) + b.astype(F32)).astype(BF16)


def gather_x(piece):
    return exchange_x(jnp.broadcast_to(piece[None], (NX,) + piece.shape))


def local(activations, enc_weight, enc_bias, dec_weight, dec_bias, thresholds, active_blocks):
    n_dp = lax.axis_size("dp")
    d = enc_weight.shape[0]
    scale_root = math.sqrt(activations.shape[0] * n_dp)
    dict_index = lax.axis_index("dict")
    core = dict_index % 2

    turned = activations.T
    halves = jnp.stack([turned[:, :TILE], turned[:, TILE:]])
    far = size_of(FAR)
    halves = jnp.broadcast_to(halves[None], (far,) + halves.shape).reshape((-1,) + halves.shape[1:])
    act = exchange(halves, FAR + CORE).reshape(far, -1, TILE)
    chip = dict_index // 2
    own = lax.dynamic_index_in_dim(act, chip // 16 * 4 + chip % 8 // 2, keepdims=False)
    cols = own.shape[0]
    act = spread(act, NEAR)

    enc_other = lax.ppermute(enc_weight, "dict", CORE_SWAP)
    dec_other = lax.ppermute(dec_weight, "dict", CORE_SWAP)
    rows = jnp.stack([enc_bias.astype(F32), thresholds.astype(F32) / 16.0])
    rows = jnp.concatenate([rows, lax.ppermute(rows, "dict", CORE_SWAP)], axis=1)
    listed = lax.dynamic_slice_in_dim(active_blocks, core, 1)
    live = jnp.stack([jnp.any(listed == dict_index), jnp.any(listed == (dict_index ^ 1))])
    live = jnp.repeat(live.astype(F32), TILE)[None, :]
    rows = jnp.concatenate([rows, live, jnp.zeros((5, 2 * TILE), F32)], axis=0)

    work = 2 * d * 2 * TILE * TILE
    parts, feat, slope = call(
        forward_kernel,
        [
            shape(act.shape),
            shape((TILE, 2 * TILE)),
            shape((TILE, 2 * TILE), F32),
        ],
        (act, enc_weight, enc_other, dec_weight, dec_other, rows),
        [pltpu.VMEM((d, TILE), BF16)],
        2 * work,
    )

    near_sum = jnp.sum(exchange(parts, NEAR).astype(F32), axis=0).astype(BF16)
    recon = jnp.sum(exchange(near_sum, FAR).astype(F32), axis=0)
    bias = lax.dynamic_slice_in_dim(dec_bias, dict_index // 2 * cols, cols).astype(F32)
    residual = (recon + bias[:, None] - own.astype(F32)) / scale_root
    res = spread(spread(residual.astype(BF16), FAR), NEAR)

    quarter = d // NX
    packed = shape((NX, quarter + DEC_BIAS_ROWS, TILE))
    room = pltpu.VMEM((d, TILE), BF16)
    dec_parts = call(
        decoder_kernel,
        [packed, packed],
        (res, feat),
        [room, pltpu.VMEM((DEC_BIAS_ROWS, TILE), F32)],
        work,
    )
    dec_parts, res = lax.optimization_barrier((dec_parts, res))
    packed = shape((NX, quarter + ENC_BIAS_ROWS, TILE))
    enc_parts = call(
        encoder_kernel,
        [packed, packed],
        (res, act, dec_weight, dec_other, slope),
        [room, room],
        2 * work,
    )

    dec_other = lax.ppermute(dec_parts[1], "dict", CORE_SWAP)
    enc_other, dec_other = lax.optimization_barrier((enc_parts[1], dec_other))
    dec_total = add(dec_parts[0], dec_other)
    enc_total = add(enc_parts[0], lax.ppermute(enc_other, "dict", CORE_SWAP))
    dec_moved, enc_total = lax.optimization_barrier((exchange_x(dec_total), enc_total))
    dec_piece = sum_parts(dec_moved)
    dec_swapped = lax.ppermute(dec_piece, "dp", Y_SWAP)
    enc_piece = sum_parts(exchange_x(enc_total))
    enc_swapped = lax.ppermute(enc_piece, "dp", Y_SWAP)
    dec_swapped, enc_piece = lax.optimization_barrier((dec_swapped, enc_piece))
    dec_sum = add(dec_piece, dec_swapped)
    dec_whole = gather_x(dec_sum[:quarter])
    (dec,) = call(unpack_kernel, [shape((TILE, d))], (dec_whole,))
    dec_whole, enc_swapped = lax.optimization_barrier((dec_whole, enc_swapped))
    enc_sum = add(enc_piece, enc_swapped)
    enc = gather_x(enc_sum[:quarter]).reshape(d, TILE)
    return enc, dec, enc_sum[quarter], dec_sum[quarter : quarter + d // TILE].reshape(-1)


def solution(mesh):
    placed = (
        P("dp", "dict"),
        P(None, "dict"),
        P("dict"),
        P("dict", None),
        P(),
        P("dict"),
        P("dp", None),
    )
    return jax.shard_map(
        local,
        mesh=mesh,
        in_specs=placed,
        out_specs=(P(None, "dict"), P("dict", None), P("dict"), P()),
        check_vma=False,
    )
```

```python
import math

import jax
import jax.numpy as jnp
import numpy as np
from jax import lax
from jax.experimental import pallas as pl
from jax.experimental.pallas import tpu as pltpu
from jax.sharding import PartitionSpec as P

TILE = 128
SHARPNESS = 4.0
F32 = jnp.float32
BF16 = jnp.bfloat16

GRID = (2, 2, 4, 2, 2)
FAR, NEAR, CORE = (0, 2), (1, 3), (4,)
CHIPS = 32
NX = 4
DEC_BIAS_ROWS, ENC_BIAS_ROWS = 48, 16
VMEM = 24 * 1024 * 1024


def size_of(axes):
    return math.prod(GRID[axis] for axis in axes)


def groups(axes):
    index = np.arange(math.prod(GRID)).reshape(GRID)
    rest = [axis for axis in range(len(GRID)) if axis not in axes]
    return index.transpose(rest + list(axes)).reshape(-1, size_of(axes)).tolist()


X_GROUPS = np.arange(8).reshape(NX, 2).T.tolist()
CORE_SWAP = [(i, i ^ 1) for i in range(64)]
Y_SWAP = [(i, i ^ 1) for i in range(8)]


def exchange(parts, axes):
    return lax.all_to_all(parts, "dict", 0, 0, axis_index_groups=groups(axes))


def spread(block, axes):
    return exchange(jnp.broadcast_to(block[None], (size_of(axes),) + block.shape), axes)


def chip_blocks():
    for near in range(4):
        for far in range(8):
            y, z = (far // 4) * 2 + near // 2, (far % 4) * 2 + near % 2
            yield near, far, y * 8 + z


def in_order(parts_ref, whole_ref):
    cols = parts_ref.shape[2]
    for near, far, chip in chip_blocks():
        whole_ref[chip * cols : (chip + 1) * cols, :] = parts_ref[near, far]


def dot(a, b, dims):
    return lax.dot_general(a, b, (dims, ((), ())), preferred_element_type=F32)


def forward_kernel(
    act_ref, we_own, we_other, wd_own, wd_other, row_ref, parts_ref, feat_ref, slope_ref, act
):
    in_order(act_ref, act)
    act_t = act[...].T
    for n, we in enumerate((we_own, we_other)):
        lanes = slice(n * TILE, (n + 1) * TILE)
        bias, theta, live = row_ref[0:1, lanes], row_ref[1:2, lanes], row_ref[2:3, lanes]
        pre = dot(act_t, we[...], ((1,), (0,))) + bias
        gate = jax.nn.sigmoid(SHARPNESS * (pre - theta))
        feat_ref[:, lanes] = (live * pre * gate).astype(BF16)
        slope_ref[lanes, :] = (live * (gate + SHARPNESS * pre * gate * (1.0 - gate))).T
    cols = parts_ref.shape[2]
    step = 8 * cols
    place = {chip: (near, far) for near, far, chip in chip_blocks()}
    for first in range(0, act.shape[0], step):
        span = slice(first, first + step)
        total = dot(feat_ref[:, :TILE], wd_own[:, span], ((1,), (0,)))
        total = total + dot(feat_ref[:, TILE:], wd_other[:, span], ((1,), (0,)))
        turned = total.astype(BF16).T
        for i in range(8):
            near, far = place[first // cols + i]
            parts_ref[near, far] = turned[i * cols : (i + 1) * cols, :]


def decoder_kernel(res_ref, feat_ref, own_ref, other_ref, res, bias):
    in_order(res_ref, res)
    d = res.shape[0]
    quarter, lat = d // NX, TILE // NX
    feat_t = jnp.concatenate([feat_ref[...].T, jnp.ones((16, TILE), BF16)], axis=0)
    bias[...] = jnp.zeros_like(bias)
    for i in range(d // TILE):
        tile = dot(feat_t, res[i * TILE : (i + 1) * TILE, :], ((1,), (1,)))
        bias[i : i + 1, :] = tile[2 * TILE : 2 * TILE + 1, :]
        tile = tile.astype(BF16)
        rows = slice(i * lat, (i + 1) * lat)
        for x in range(NX):
            own_ref[x, rows, :] = tile[x * lat : (x + 1) * lat, :]
            other_ref[x, rows, :] = tile[TILE + x * lat : TILE + (x + 1) * lat, :]
    rows = bias[...].astype(BF16)
    for x in range(NX):
        own_ref[x, quarter:, :] = rows
        other_ref[x, quarter:, :] = rows


def encoder_kernel(
    res_ref, act_ref, wd_own, wd_other, slope_ref, own_ref, other_ref, act, res
):
    in_order(act_ref, act)
    in_order(res_ref, res)
    quarter = act.shape[0] // NX
    for n, (wd, out) in enumerate(((wd_own, own_ref), (wd_other, other_ref))):
        dfeat = dot(wd[...], res[...], ((1,), (0,)))
        dpre = (dfeat * slope_ref[n * TILE : (n + 1) * TILE, :]).T
        row = jnp.sum(dpre, axis=0, keepdims=True)
        rows = jnp.broadcast_to(row, (ENC_BIAS_ROWS, TILE)).astype(BF16)
        dpre = dpre.astype(BF16)
        for x in range(NX):
            enc = dot(act[x * quarter : (x + 1) * quarter, :], dpre, ((1,), (0,)))
            out[x, :quarter, :] = enc.astype(BF16)
            out[x, quarter:, :] = rows


def unpack_kernel(parts_ref, dec_ref):
    lat = dec_ref.shape[0] // NX
    for x in range(NX):
        for i in range(dec_ref.shape[1] // TILE):
            rows, lanes = slice(i * lat, (i + 1) * lat), slice(i * TILE, (i + 1) * TILE)
            dec_ref[x * lat : (x + 1) * lat, lanes] = parts_ref[x, rows, :]


def call(kernel, outs, args, scratch=(), flops=0):
    whole = pl.BlockSpec(memory_space=pltpu.VMEM)
    moved = sum(a.size * a.dtype.itemsize for a in args)
    moved += sum(math.prod(s.shape) * s.dtype.itemsize for s in outs)
    return pl.pallas_call(
        kernel,
        out_shape=outs,
        in_specs=[whole] * len(args),
        out_specs=[whole] * len(outs),
        scratch_shapes=list(scratch),
        compiler_params=pltpu.CompilerParams(vmem_limit_bytes=VMEM),
        cost_estimate=pl.CostEstimate(flops=flops, bytes_accessed=moved, transcendentals=0),
    )(*args)


def shape(dims, dtype=BF16):
    return jax.ShapeDtypeStruct(dims, dtype)


def exchange_x(parts):
    return lax.all_to_all(parts, "dp", 0, 0, axis_index_groups=X_GROUPS)


def sum_parts(parts):
    return lax.optimization_barrier(jnp.sum(parts.astype(F32), axis=0).astype(BF16))


def add(a, b):
    return (a.astype(F32) + b.astype(F32)).astype(BF16)


def gather_x(piece):
    return exchange_x(jnp.broadcast_to(piece[None], (NX,) + piece.shape))


def local(activations, enc_weight, enc_bias, dec_weight, dec_bias, thresholds, active_blocks):
    n_dp = lax.axis_size("dp")
    d = enc_weight.shape[0]
    scale_root = math.sqrt(activations.shape[0] * n_dp)
    dict_index = lax.axis_index("dict")
    core = dict_index % 2

    turned = activations.T
    halves = jnp.stack([turned[:, :TILE], turned[:, TILE:]])
    far = size_of(FAR)
    halves = jnp.broadcast_to(halves[None], (far,) + halves.shape).reshape((-1,) + halves.shape[1:])
    act = exchange(halves, FAR + CORE).reshape(far, -1, TILE)
    chip = dict_index // 2
    own = lax.dynamic_index_in_dim(act, chip // 16 * 4 + chip % 8 // 2, keepdims=False)
    cols = own.shape[0]
    act = spread(act, NEAR)

    enc_other = lax.ppermute(enc_weight, "dict", CORE_SWAP)
    dec_other = lax.ppermute(dec_weight, "dict", CORE_SWAP)
    rows = jnp.stack([enc_bias.astype(F32), thresholds.astype(F32) / 16.0])
    rows = jnp.concatenate([rows, lax.ppermute(rows, "dict", CORE_SWAP)], axis=1)
    listed = lax.dynamic_slice_in_dim(active_blocks, core, 1)
    live = jnp.stack([jnp.any(listed == dict_index), jnp.any(listed == (dict_index ^ 1))])
    live = jnp.repeat(live.astype(F32), TILE)[None, :]
    rows = jnp.concatenate([rows, live, jnp.zeros((5, 2 * TILE), F32)], axis=0)

    work = 2 * d * 2 * TILE * TILE
    parts, feat, slope = call(
        forward_kernel,
        [
            shape(act.shape),
            shape((TILE, 2 * TILE)),
            shape((2 * TILE, TILE), F32),
        ],
        (act, enc_weight, enc_other, dec_weight, dec_other, rows),
        [pltpu.VMEM((d, TILE), BF16)],
        2 * work,
    )

    near_sum = jnp.sum(exchange(parts, NEAR).astype(F32), axis=0).astype(BF16)
    recon = jnp.sum(exchange(near_sum, FAR).astype(F32), axis=0)
    bias = lax.dynamic_slice_in_dim(dec_bias, dict_index // 2 * cols, cols).astype(F32)
    residual = (recon + bias[:, None] - own.astype(F32)) / scale_root
    res = spread(spread(residual.astype(BF16), FAR), NEAR)

    quarter = d // NX
    packed = shape((NX, quarter + DEC_BIAS_ROWS, TILE))
    room = pltpu.VMEM((d, TILE), BF16)
    dec_parts = call(
        decoder_kernel,
        [packed, packed],
        (res, feat),
        [room, pltpu.VMEM((DEC_BIAS_ROWS, TILE), F32)],
        work,
    )
    dec_parts, res = lax.optimization_barrier((dec_parts, res))
    packed = shape((NX, quarter + ENC_BIAS_ROWS, TILE))
    enc_parts = call(
        encoder_kernel,
        [packed, packed],
        (res, act, dec_weight, dec_other, slope),
        [room, room],
        2 * work,
    )

    dec_other = lax.ppermute(dec_parts[1], "dict", CORE_SWAP)
    dec_total = add(dec_parts[0], dec_other)
    enc_other, dec_total = lax.optimization_barrier((enc_parts[1], dec_total))
    enc_total = add(enc_parts[0], lax.ppermute(enc_other, "dict", CORE_SWAP))
    dec_moved, enc_total = lax.optimization_barrier((exchange_x(dec_total), enc_total))
    dec_piece = sum_parts(dec_moved)
    dec_swapped = lax.ppermute(dec_piece, "dp", Y_SWAP)
    enc_piece = sum_parts(exchange_x(enc_total))
    enc_swapped = lax.ppermute(enc_piece, "dp", Y_SWAP)
    dec_swapped, enc_piece = lax.optimization_barrier((dec_swapped, enc_piece))
    dec_sum = add(dec_piece, dec_swapped)
    dec_whole = gather_x(dec_sum[:quarter])
    (dec,) = call(unpack_kernel, [shape((TILE, d))], (dec_whole,))
    dec_whole, enc_swapped = lax.optimization_barrier((dec_whole, enc_swapped))
    enc_sum = add(enc_piece, enc_swapped)
    enc = gather_x(enc_sum[:quarter]).reshape(d, TILE)
    return enc, dec, enc_sum[quarter], dec_sum[quarter : quarter + d // TILE].reshape(-1)


def solution(mesh):
    placed = (
        P("dp", "dict"),
        P(None, "dict"),
        P("dict"),
        P("dict", None),
        P(),
        P("dict"),
        P("dp", None),
    )
    return jax.shard_map(
        local,
        mesh=mesh,
        in_specs=placed,
        out_specs=(P(None, "dict"), P("dict", None), P("dict"), P()),
        check_vma=False,
    )
```

```python
import math

import jax
import jax.numpy as jnp
import numpy as np
from jax import lax
from jax.experimental import pallas as pl
from jax.experimental.pallas import tpu as pltpu
from jax.sharding import PartitionSpec as P

TILE = 128
SHARPNESS = 4.0
F32 = jnp.float32
BF16 = jnp.bfloat16

GRID = (2, 2, 4, 2, 2)
FAR, NEAR, CORE = (0, 2), (1, 3), (4,)
CHIPS = 32
NX = 4
DEC_BIAS_ROWS, ENC_BIAS_ROWS = 48, 16
VMEM = 48 * 1024 * 1024


def size_of(axes):
    return math.prod(GRID[axis] for axis in axes)


def groups(axes):
    index = np.arange(math.prod(GRID)).reshape(GRID)
    rest = [axis for axis in range(len(GRID)) if axis not in axes]
    return index.transpose(rest + list(axes)).reshape(-1, size_of(axes)).tolist()


ALL = ("dict", "dp")


def along_x(sign):
    pairs = []
    for d in range(64):
        step = sign * (1 - 2 * (d % 2))
        for x in range(NX):
            pairs += [(d * 8 + x * 2 + h, d * 8 + (x + step) % NX * 2 + h) for h in range(2)]
    return pairs


AHEAD, BACK = along_x(1), along_x(-1)
CORE_SWAP = [(i, i ^ 1) for i in range(64)]
Y_SWAP = [(i, i ^ 1) for i in range(8)]


def exchange(parts, axes):
    return lax.all_to_all(parts, "dict", 0, 0, axis_index_groups=groups(axes))


def spread(block, axes):
    return exchange(jnp.broadcast_to(block[None], (size_of(axes),) + block.shape), axes)


def chip_blocks():
    for near in range(4):
        for far in range(8):
            y, z = (far // 4) * 2 + near // 2, (far % 4) * 2 + near % 2
            yield near, far, y * 8 + z


def in_order(parts_ref, whole_ref):
    cols = parts_ref.shape[2]
    for near, far, chip in chip_blocks():
        whole_ref[chip * cols : (chip + 1) * cols, :] = parts_ref[near, far]


def dot(a, b, dims):
    return lax.dot_general(a, b, (dims, ((), ())), preferred_element_type=F32)


def forward_kernel(
    act_ref, we_own, we_other, wd_own, wd_other, row_ref, parts_ref, feat_ref, slope_ref, act
):
    in_order(act_ref, act)
    act_t = act[...].T
    for n, we in enumerate((we_own, we_other)):
        lanes = slice(n * TILE, (n + 1) * TILE)
        bias, theta, live = row_ref[0:1, lanes], row_ref[1:2, lanes], row_ref[2:3, lanes]
        pre = dot(act_t, we[...], ((1,), (0,))) + bias
        gate = jax.nn.sigmoid(SHARPNESS * (pre - theta))
        feat_ref[:, lanes] = (live * pre * gate).astype(BF16)
        slope_ref[lanes, :] = (live * (gate + SHARPNESS * pre * gate * (1.0 - gate))).T
    cols = parts_ref.shape[2]
    step = 8 * cols
    place = {chip: (near, far) for near, far, chip in chip_blocks()}
    for first in range(0, act.shape[0], step):
        span = slice(first, first + step)
        total = dot(feat_ref[:, :TILE], wd_own[:, span], ((1,), (0,)))
        total = total + dot(feat_ref[:, TILE:], wd_other[:, span], ((1,), (0,)))
        turned = total.astype(BF16).T
        for i in range(8):
            near, far = place[first // cols + i]
            parts_ref[near, far] = turned[i * cols : (i + 1) * cols, :]


def decoder_kernel(res_ref, feat_ref, own_ref, other_ref, res, bias):
    in_order(res_ref, res)
    d = res.shape[0]
    quarter, lat = d // NX, TILE // NX
    feat_t = jnp.concatenate([feat_ref[...].T, jnp.ones((16, TILE), BF16)], axis=0)
    bias[...] = jnp.zeros_like(bias)
    for i in range(d // TILE):
        tile = dot(feat_t, res[i * TILE : (i + 1) * TILE, :], ((1,), (1,)))
        bias[i : i + 1, :] = tile[2 * TILE : 2 * TILE + 1, :]
        tile = tile.astype(BF16)
        rows = slice(i * lat, (i + 1) * lat)
        for x in range(NX):
            own_ref[x, rows, :] = tile[x * lat : (x + 1) * lat, :]
            other_ref[x, rows, :] = tile[TILE + x * lat : TILE + (x + 1) * lat, :]
    rows = bias[...].astype(BF16)
    for x in range(NX):
        own_ref[x, quarter:, :] = rows
        other_ref[x, quarter:, :] = rows


def encoder_kernel(
    res_ref, act_ref, wd_own, wd_other, slope_ref, own_ref, other_ref, act, res
):
    in_order(act_ref, act)
    in_order(res_ref, res)
    quarter = act.shape[0] // NX
    for n, (wd, out) in enumerate(((wd_own, own_ref), (wd_other, other_ref))):
        dfeat = dot(wd[...], res[...], ((1,), (0,)))
        dpre = (dfeat * slope_ref[n * TILE : (n + 1) * TILE, :]).T
        row = jnp.sum(dpre, axis=0, keepdims=True)
        rows = jnp.broadcast_to(row, (ENC_BIAS_ROWS, TILE)).astype(BF16)
        dpre = dpre.astype(BF16)
        for x in range(NX):
            enc = dot(act[x * quarter : (x + 1) * quarter, :], dpre, ((1,), (0,)))
            out[x, :quarter, :] = enc.astype(BF16)
            out[x, quarter:, :] = rows


def place_dec_kernel(order_ref, *refs):
    dec_ref = refs[-1]
    lat = dec_ref.shape[0] // NX
    for n, ref in enumerate(refs[:-1]):
        row = pl.multiple_of(order_ref[n] * lat, lat)
        for i in range(dec_ref.shape[1] // TILE):
            lanes = slice(i * TILE, (i + 1) * TILE)
            dec_ref[pl.ds(row, lat), lanes] = ref[i * lat : (i + 1) * lat, :]


def place_enc_kernel(order_ref, *refs):
    enc_ref = refs[-1]
    quarter = enc_ref.shape[0] // NX
    for n, ref in enumerate(refs[:-1]):
        row = pl.multiple_of(order_ref[n] * quarter, quarter)
        enc_ref[pl.ds(row, quarter), :] = ref[:quarter, :]


def call(kernel, outs, args, scratch=(), flops=0):
    whole = pl.BlockSpec(memory_space=pltpu.VMEM)
    scalars = pl.BlockSpec(memory_space=pltpu.SMEM)
    moved = sum(a.size * a.dtype.itemsize for a in args)
    moved += sum(math.prod(s.shape) * s.dtype.itemsize for s in outs)
    return pl.pallas_call(
        kernel,
        out_shape=outs,
        in_specs=[scalars if a.dtype == jnp.int32 else whole for a in args],
        out_specs=[whole] * len(outs),
        scratch_shapes=list(scratch),
        compiler_params=pltpu.CompilerParams(vmem_limit_bytes=VMEM),
        cost_estimate=pl.CostEstimate(flops=flops, bytes_accessed=moved, transcendentals=0),
    )(*args)


def shape(dims, dtype=BF16):
    return jax.ShapeDtypeStruct(dims, dtype)


def add(*terms):
    return sum(term.astype(F32) for term in terms).astype(BF16)


def scatter_x(own, other, ahead, back, x):
    def quarter(n):
        return [lax.dynamic_index_in_dim(part, n, keepdims=False) for part in (own, other)]

    relayed = lax.ppermute(add(*quarter((x + 2) % NX)), ALL, AHEAD)
    direct = lax.ppermute(add(*quarter(back)), ALL, BACK)
    passed = lax.ppermute(add(*quarter(ahead), relayed), ALL, AHEAD)
    return lax.optimization_barrier(add(*quarter(x), direct, passed))


def gather_x(piece):
    behind = lax.ppermute(piece, ALL, AHEAD)
    ahead = lax.ppermute(piece, ALL, BACK)
    return piece, behind, ahead, lax.ppermute(behind, ALL, AHEAD)


def local(activations, enc_weight, enc_bias, dec_weight, dec_bias, thresholds, active_blocks):
    n_dp = lax.axis_size("dp")
    d = enc_weight.shape[0]
    scale_root = math.sqrt(activations.shape[0] * n_dp)
    dict_index = lax.axis_index("dict")
    core = dict_index % 2

    turned = activations.T
    halves = jnp.stack([turned[:, :TILE], turned[:, TILE:]])
    far = size_of(FAR)
    halves = jnp.broadcast_to(halves[None], (far,) + halves.shape).reshape((-1,) + halves.shape[1:])
    act = exchange(halves, FAR + CORE).reshape(far, -1, TILE)
    chip = dict_index // 2
    own = lax.dynamic_index_in_dim(act, chip // 16 * 4 + chip % 8 // 2, keepdims=False)
    cols = own.shape[0]
    act = spread(act, NEAR)

    enc_other = lax.ppermute(enc_weight, "dict", CORE_SWAP)
    dec_other = lax.ppermute(dec_weight, "dict", CORE_SWAP)
    rows = jnp.stack([enc_bias.astype(F32), thresholds.astype(F32) / 16.0])
    rows = jnp.concatenate([rows, lax.ppermute(rows, "dict", CORE_SWAP)], axis=1)
    listed = lax.dynamic_slice_in_dim(active_blocks, core, 1)
    live = jnp.stack([jnp.any(listed == dict_index), jnp.any(listed == (dict_index ^ 1))])
    live = jnp.repeat(live.astype(F32), TILE)[None, :]
    rows = jnp.concatenate([rows, live, jnp.zeros((5, 2 * TILE), F32)], axis=0)

    work = 2 * d * 2 * TILE * TILE
    parts, feat, slope = call(
        forward_kernel,
        [
            shape(act.shape),
            shape((TILE, 2 * TILE)),
            shape((2 * TILE, TILE), F32),
        ],
        (act, enc_weight, enc_other, dec_weight, dec_other, rows),
        [pltpu.VMEM((d, TILE), BF16)],
        2 * work,
    )

    near_sum = jnp.sum(exchange(parts, NEAR).astype(F32), axis=0).astype(BF16)
    recon = jnp.sum(exchange(near_sum, FAR).astype(F32), axis=0)
    bias = lax.dynamic_slice_in_dim(dec_bias, dict_index // 2 * cols, cols).astype(F32)
    residual = (recon + bias[:, None] - own.astype(F32)) / scale_root
    res = spread(spread(residual.astype(BF16), FAR), NEAR)

    quarter = d // NX
    packed = shape((NX, quarter + DEC_BIAS_ROWS, TILE))
    room = pltpu.VMEM((d, TILE), BF16)
    dec_parts = call(
        decoder_kernel,
        [packed, packed],
        (res, feat),
        [room, pltpu.VMEM((DEC_BIAS_ROWS, TILE), F32)],
        work,
    )
    dec_parts, res = lax.optimization_barrier((dec_parts, res))
    packed = shape((NX, quarter + ENC_BIAS_ROWS, TILE))
    enc_parts = call(
        encoder_kernel,
        [packed, packed],
        (res, act, dec_weight, dec_other, slope),
        [room, room],
        2 * work,
    )

    x = lax.axis_index("dp") // 2
    ahead, back = (x + 1 + 2 * core) % NX, (x + 3 + 2 * core) % NX
    order = jnp.stack([x, back, ahead, (x + 2) % NX]).astype(jnp.int32)
    dec_other = lax.ppermute(dec_parts[1], "dict", CORE_SWAP)
    enc_other, dec_other = lax.optimization_barrier((enc_parts[1], dec_other))
    enc_other = lax.ppermute(enc_other, "dict", CORE_SWAP)
    dec_piece = scatter_x(dec_parts[0], dec_other, ahead, back, x)
    enc_piece = scatter_x(enc_parts[0], enc_other, ahead, back, x)
    dec_piece = add(dec_piece, lax.ppermute(dec_piece, "dp", Y_SWAP))
    enc_piece = add(enc_piece, lax.ppermute(enc_piece, "dp", Y_SWAP))
    (dec,) = call(place_dec_kernel, [shape((TILE, d))], (order, *gather_x(dec_piece)))
    (enc,) = call(place_enc_kernel, [shape((d, TILE))], (order, *gather_x(enc_piece)))
    return enc, dec, enc_piece[quarter], dec_piece[quarter : quarter + d // TILE].reshape(-1)


def solution(mesh):
    placed = (
        P("dp", "dict"),
        P(None, "dict"),
        P("dict"),
        P("dict", None),
        P(),
        P("dict"),
        P("dp", None),
    )
    return jax.shard_map(
        local,
        mesh=mesh,
        in_specs=placed,
        out_specs=(P(None, "dict"), P("dict", None), P("dict"), P()),
        check_vma=False,
    )
```

```python
import math

import jax
import jax.numpy as jnp
import numpy as np
from jax import lax
from jax.experimental import pallas as pl
from jax.experimental.pallas import tpu as pltpu
from jax.sharding import PartitionSpec as P

TILE = 128
SHARPNESS = 4.0
F32 = jnp.float32
BF16 = jnp.bfloat16

GRID = (2, 2, 4, 2, 2)
FAR, CORE = (0, 2), (4,)
NX = 4
DEC_BIAS_ROWS, ENC_BIAS_ROWS = 48, 16
VMEM = 24 * 1024 * 1024


def size_of(axes):
    return math.prod(GRID[axis] for axis in axes)


def groups(axes):
    index = np.arange(math.prod(GRID)).reshape(GRID)
    rest = [axis for axis in range(len(GRID)) if axis not in axes]
    return index.transpose(rest + list(axes)).reshape(-1, size_of(axes)).tolist()


ALL = ("dict", "dp")


def along_x(sign):
    pairs = []
    for d in range(64):
        step = sign * (1 - 2 * (d % 2))
        for x in range(NX):
            pairs += [(d * 8 + x * 2 + h, d * 8 + (x + step) % NX * 2 + h) for h in range(2)]
    return pairs


AHEAD, BACK = along_x(1), along_x(-1)
CORE_SWAP = [(i, i ^ 1) for i in range(64)]
Y_SWAP = [(i, i ^ 1) for i in range(8)]


def exchange(parts, axes):
    return lax.all_to_all(parts, "dict", 0, 0, axis_index_groups=groups(axes))


NEAR_A = [(d, d ^ (2 if d % 2 else 16)) for d in range(64)]
NEAR_B = [(d, d ^ (16 if d % 2 else 2)) for d in range(64)]


def gather_near(block):
    first = lax.ppermute(block, "dict", NEAR_A)
    second = lax.ppermute(block, "dict", NEAR_B)
    return block, first, second, lax.ppermute(first, "dict", NEAR_B)


def scatter_near(own, first, second, opposite):
    relayed = lax.ppermute(opposite, "dict", NEAR_A)
    direct = lax.ppermute(first, "dict", NEAR_A)
    passed = lax.ppermute(add(second, relayed), "dict", NEAR_B)
    return add(own, direct, passed)


def add(*terms):
    return sum(term.astype(F32) for term in terms).astype(BF16)


def spread(block, axes):
    return exchange(jnp.broadcast_to(block[None], (size_of(axes),) + block.shape), axes)


def chip_rows(near_ref, cols):
    for n in range(4):
        near = near_ref[n]
        for far in range(8):
            chip = far // 4 * 16 + near // 2 * 8 + far % 4 * 2 + near % 2
            yield n, far, pl.multiple_of(chip * cols, cols)


def in_order(near_ref, refs, whole_ref):
    cols = refs[0].shape[1]
    for n, far, row in chip_rows(near_ref, cols):
        whole_ref[pl.ds(row, cols), :] = refs[n][far]


def dot(a, b, dims):
    return lax.dot_general(a, b, (dims, ((), ())), preferred_element_type=F32)


def forward_kernel(
    near_ref, act_0, act_1, act_2, act_3, we_own, we_other, wd_own, wd_other, row_ref,
    part_0, part_1, part_2, part_3, feat_ref, slope_ref, act, parts,
):
    in_order(near_ref, (act_0, act_1, act_2, act_3), act)
    act_t = act[...].T
    for n, we in enumerate((we_own, we_other)):
        lanes = slice(n * TILE, (n + 1) * TILE)
        bias, theta, live = row_ref[0:1, lanes], row_ref[1:2, lanes], row_ref[2:3, lanes]
        pre = dot(act_t, we[...], ((1,), (0,))) + bias
        gate = jax.nn.sigmoid(SHARPNESS * (pre - theta))
        feat_ref[:, lanes] = (live * pre * gate).astype(BF16)
        slope_ref[lanes, :] = (live * (gate + SHARPNESS * pre * gate * (1.0 - gate))).T
    step = 9 * TILE
    for at in range(0, act.shape[0], step):
        span = slice(at, at + step)
        total = dot(feat_ref[:, :TILE], wd_own[:, span], ((1,), (0,)))
        total = total + dot(feat_ref[:, TILE:], wd_other[:, span], ((1,), (0,)))
        parts[span, :] = total.astype(BF16).T
    cols = part_0.shape[1]
    for n, far, row in chip_rows(near_ref, cols):
        (part_0, part_1, part_2, part_3)[n][far] = parts[pl.ds(row, cols), :]


def decoder_kernel(
    near_ref, res_0, res_1, res_2, res_3, feat_ref, own_ref, other_ref, res, bias
):
    in_order(near_ref, (res_0, res_1, res_2, res_3), res)
    d = res.shape[0]
    quarter, lat = d // NX, TILE // NX
    feat_t = jnp.concatenate([feat_ref[...].T, jnp.ones((16, TILE), BF16)], axis=0)
    bias[...] = jnp.zeros_like(bias)
    for i in range(d // TILE):
        tile = dot(feat_t, res[i * TILE : (i + 1) * TILE, :], ((1,), (1,)))
        bias[i : i + 1, :] = tile[2 * TILE : 2 * TILE + 1, :]
        tile = tile.astype(BF16)
        rows = slice(i * lat, (i + 1) * lat)
        for x in range(NX):
            own_ref[x, rows, :] = tile[x * lat : (x + 1) * lat, :]
            other_ref[x, rows, :] = tile[TILE + x * lat : TILE + (x + 1) * lat, :]
    rows = bias[...].astype(BF16)
    for x in range(NX):
        own_ref[x, quarter:, :] = rows
        other_ref[x, quarter:, :] = rows


def encoder_kernel(
    near_ref, res_0, res_1, res_2, res_3, act_0, act_1, act_2, act_3, wd_own, wd_other, slope_ref,
    own_ref, other_ref, act, res,
):
    in_order(near_ref, (act_0, act_1, act_2, act_3), act)
    in_order(near_ref, (res_0, res_1, res_2, res_3), res)
    quarter = act.shape[0] // NX
    for n, (wd, out) in enumerate(((wd_own, own_ref), (wd_other, other_ref))):
        dfeat = dot(wd[...], res[...], ((1,), (0,)))
        dpre = (dfeat * slope_ref[n * TILE : (n + 1) * TILE, :]).T
        row = jnp.sum(dpre, axis=0, keepdims=True)
        rows = jnp.broadcast_to(row, (ENC_BIAS_ROWS, TILE)).astype(BF16)
        dpre = dpre.astype(BF16)
        for x in range(NX):
            enc = dot(act[x * quarter : (x + 1) * quarter, :], dpre, ((1,), (0,)))
            out[x, :quarter, :] = enc.astype(BF16)
            out[x, quarter:, :] = rows


def place_dec_kernel(order_ref, *refs):
    dec_ref = refs[-1]
    lat = dec_ref.shape[0] // NX
    for n, ref in enumerate(refs[:-1]):
        row = pl.multiple_of(order_ref[n] * lat, lat)
        for i in range(dec_ref.shape[1] // TILE):
            lanes = slice(i * TILE, (i + 1) * TILE)
            dec_ref[pl.ds(row, lat), lanes] = ref[i * lat : (i + 1) * lat, :]


def place_enc_kernel(order_ref, *refs):
    enc_ref = refs[-1]
    quarter = enc_ref.shape[0] // NX
    for n, ref in enumerate(refs[:-1]):
        row = pl.multiple_of(order_ref[n] * quarter, quarter)
        enc_ref[pl.ds(row, quarter), :] = ref[:quarter, :]


def call(kernel, outs, args, scratch=(), flops=0):
    whole = pl.BlockSpec(memory_space=pltpu.VMEM)
    scalars = pl.BlockSpec(memory_space=pltpu.SMEM)
    moved = sum(a.size * a.dtype.itemsize for a in args)
    moved += sum(math.prod(s.shape) * s.dtype.itemsize for s in outs)
    return pl.pallas_call(
        kernel,
        out_shape=outs,
        in_specs=[scalars if a.dtype == jnp.int32 else whole for a in args],
        out_specs=[whole] * len(outs),
        scratch_shapes=list(scratch),
        compiler_params=pltpu.CompilerParams(vmem_limit_bytes=VMEM),
        cost_estimate=pl.CostEstimate(flops=flops, bytes_accessed=moved, transcendentals=0),
    )(*args)


def shape(dims, dtype=BF16):
    return jax.ShapeDtypeStruct(dims, dtype)


def after(value, *others):
    return lax.optimization_barrier((value, *others))[0]


def gather_x(piece, *first):
    behind = lax.ppermute(piece, ALL, AHEAD)
    ahead = lax.ppermute(after(piece, *first), ALL, BACK)
    return piece, behind, ahead, lax.ppermute(behind, ALL, AHEAD)


def quarter_of(parts, n):
    return [lax.dynamic_index_in_dim(part, n, keepdims=False) for part in parts]


def reduce_gradients(dec, enc, core, x):
    ahead, back = (x + 1 + 2 * core) % NX, (x + 3 + 2 * core) % NX
    dec = dec[0], lax.ppermute(dec[1], "dict", CORE_SWAP)
    enc = enc[0], lax.ppermute(after(enc[1], dec[1]), "dict", CORE_SWAP)

    relayed = lax.ppermute(add(*quarter_of(dec, (x + 2) % NX)), ALL, AHEAD)
    direct = lax.ppermute(add(*quarter_of(dec, back)), ALL, BACK)
    passed = lax.ppermute(add(*quarter_of(dec, ahead), relayed), ALL, AHEAD)
    dec_piece = lax.optimization_barrier(add(*quarter_of(dec, x), direct, passed))
    dec_swapped = lax.ppermute(dec_piece, "dp", Y_SWAP)

    relayed = lax.ppermute(after(add(*quarter_of(enc, (x + 2) % NX)), direct), ALL, AHEAD)
    direct = lax.ppermute(after(add(*quarter_of(enc, back)), dec_piece), ALL, BACK)
    passed = lax.ppermute(add(*quarter_of(enc, ahead), relayed), ALL, AHEAD)
    enc_piece = lax.optimization_barrier(add(*quarter_of(enc, x), direct, passed))
    enc_swapped = lax.ppermute(after(enc_piece, dec_swapped), "dp", Y_SWAP)

    dec_pieces = gather_x(add(dec_piece, dec_swapped))
    enc_swapped = after(enc_swapped, *dec_pieces[1:3])
    enc_pieces = gather_x(add(enc_piece, enc_swapped), dec_pieces[3])
    return dec_pieces, enc_pieces, jnp.stack([x, back, ahead, (x + 2) % NX]).astype(jnp.int32)


def local(activations, enc_weight, enc_bias, dec_weight, dec_bias, thresholds, active_blocks):
    n_dp = lax.axis_size("dp")
    d = enc_weight.shape[0]
    scale_root = math.sqrt(activations.shape[0] * n_dp)
    dict_index = lax.axis_index("dict")
    core = dict_index % 2

    turned = activations.T
    halves = jnp.stack([turned[:, :TILE], turned[:, TILE:]])
    far = size_of(FAR)
    halves = jnp.broadcast_to(halves[None], (far,) + halves.shape).reshape((-1,) + halves.shape[1:])
    act = exchange(halves, FAR + CORE).reshape(far, -1, TILE)
    chip = dict_index // 2
    own = lax.dynamic_index_in_dim(act, chip // 16 * 4 + chip % 8 // 2, keepdims=False)
    cols = own.shape[0]
    near = chip // 8 % 2 * 2 + chip % 2
    toward = 2 - core
    nears = jnp.stack([near, near ^ toward, near ^ (3 - toward), near ^ 3]).astype(jnp.int32)

    enc_other = lax.ppermute(after(enc_weight, halves), "dict", CORE_SWAP)
    dec_other = lax.ppermute(after(dec_weight, halves), "dict", CORE_SWAP)
    rows = jnp.stack([enc_bias.astype(F32), thresholds.astype(F32) / 16.0])
    rows = jnp.concatenate([rows, lax.ppermute(rows, "dict", CORE_SWAP)], axis=1)
    listed = lax.dynamic_slice_in_dim(active_blocks, core, 1)
    live = jnp.stack([jnp.any(listed == dict_index), jnp.any(listed == (dict_index ^ 1))])
    live = jnp.repeat(live.astype(F32), TILE)[None, :]
    rows = jnp.concatenate([rows, live, jnp.zeros((5, 2 * TILE), F32)], axis=0)

    act, rows = lax.optimization_barrier((act, rows))
    act = gather_near(act)

    work = 2 * d * 2 * TILE * TILE
    *parts, feat, slope = call(
        forward_kernel,
        [
            *[shape(act[0].shape)] * 4,
            shape((TILE, 2 * TILE)),
            shape((2 * TILE, TILE), F32),
        ],
        (nears, *act, enc_weight, enc_other, dec_weight, dec_other, rows),
        [pltpu.VMEM((d, TILE), BF16)] * 2,
        2 * work,
    )

    recon = jnp.sum(exchange(scatter_near(*parts), FAR).astype(F32), axis=0)
    bias = lax.dynamic_slice_in_dim(dec_bias, dict_index // 2 * cols, cols).astype(F32)
    residual = (recon + bias[:, None] - own.astype(F32)) / scale_root
    res = gather_near(spread(residual.astype(BF16), FAR))

    quarter = d // NX
    packed = shape((NX, quarter + DEC_BIAS_ROWS, TILE))
    room = pltpu.VMEM((d, TILE), BF16)
    dec_parts = call(
        decoder_kernel,
        [packed, packed],
        (nears, *res, feat),
        [room, pltpu.VMEM((DEC_BIAS_ROWS, TILE), F32)],
        work,
    )
    dec_parts, res = lax.optimization_barrier((dec_parts, res))
    packed = shape((NX, quarter + ENC_BIAS_ROWS, TILE))
    enc_parts = call(
        encoder_kernel,
        [packed, packed],
        (nears, *res, *act, dec_weight, dec_other, slope),
        [room, room],
        2 * work,
    )

    x = lax.axis_index("dp") // 2
    dec_pieces, enc_pieces, order = reduce_gradients(dec_parts, enc_parts, core, x)
    (dec,) = call(place_dec_kernel, [shape((TILE, d))], (order, *dec_pieces))
    (enc,) = call(place_enc_kernel, [shape((d, TILE))], (order, *enc_pieces))
    dec_bias_sum = dec_pieces[0][quarter : quarter + d // TILE].reshape(-1)
    return enc, dec, enc_pieces[0][quarter], dec_bias_sum


def solution(mesh):
    placed = (
        P("dp", "dict"),
        P(None, "dict"),
        P("dict"),
        P("dict", None),
        P(),
        P("dict"),
        P("dp", None),
    )
    return jax.shard_map(
        local,
        mesh=mesh,
        in_specs=placed,
        out_specs=(P(None, "dict"), P("dict", None), P("dict"), P()),
        check_vma=False,
    )
```

```python
import math

import jax
import jax.numpy as jnp
import numpy as np
from jax import lax
from jax.experimental import pallas as pl
from jax.experimental.pallas import tpu as pltpu
from jax.sharding import PartitionSpec as P

TILE = 128
SHARPNESS = 4.0
F32 = jnp.float32
BF16 = jnp.bfloat16

GRID = (2, 2, 4, 2, 2)
FAR, CORE = (0, 2), (4,)
NX = 4
DEC_BIAS_ROWS, ENC_BIAS_ROWS = 48, 16
VMEM = 48 * 1024 * 1024


def size_of(axes):
    return math.prod(GRID[axis] for axis in axes)


def groups(axes):
    index = np.arange(math.prod(GRID)).reshape(GRID)
    rest = [axis for axis in range(len(GRID)) if axis not in axes]
    return index.transpose(rest + list(axes)).reshape(-1, size_of(axes)).tolist()


ALL = ("dict", "dp")


def along_x(sign):
    pairs = []
    for d in range(64):
        step = sign * (1 - 2 * (d % 2))
        for x in range(NX):
            pairs += [(d * 8 + x * 2 + h, d * 8 + (x + step) % NX * 2 + h) for h in range(2)]
    return pairs


X_GROUPS = np.arange(8).reshape(NX, 2).T.tolist()
AHEAD, BACK = along_x(1), along_x(-1)
CORE_SWAP = [(i, i ^ 1) for i in range(64)]
Y_SWAP = [(i, i ^ 1) for i in range(8)]


def exchange(parts, axes):
    return lax.all_to_all(parts, "dict", 0, 0, axis_index_groups=groups(axes))


NEAR_A = [(d, d ^ (2 if d % 2 else 16)) for d in range(64)]
NEAR_B = [(d, d ^ (16 if d % 2 else 2)) for d in range(64)]


def gather_near(block):
    first = lax.ppermute(block, "dict", NEAR_A)
    second = lax.ppermute(block, "dict", NEAR_B)
    return block, first, second, lax.ppermute(first, "dict", NEAR_B)


def scatter_near(own, first, second, opposite):
    relayed = lax.ppermute(opposite, "dict", NEAR_A)
    direct = lax.ppermute(first, "dict", NEAR_A)
    passed = lax.ppermute(add(second, relayed), "dict", NEAR_B)
    return add(own, direct, passed)


def add(*terms):
    return sum(term.astype(F32) for term in terms).astype(BF16)


def spread(block, axes):
    return exchange(jnp.broadcast_to(block[None], (size_of(axes),) + block.shape), axes)


def chip_rows(near_ref, cols):
    for n in range(4):
        near = near_ref[n]
        for far in range(8):
            chip = far // 4 * 16 + near // 2 * 8 + far % 4 * 2 + near % 2
            yield n, far, pl.multiple_of(chip * cols, cols)


def in_order(near_ref, refs, whole_ref):
    cols = refs[0].shape[1]
    for n, far, row in chip_rows(near_ref, cols):
        whole_ref[pl.ds(row, cols), :] = refs[n][far]


def dot(a, b, dims):
    return lax.dot_general(a, b, (dims, ((), ())), preferred_element_type=F32)


def forward_kernel(
    near_ref, act_0, act_1, act_2, act_3, we_own, we_other, wd_own, wd_other, row_ref,
    part_0, part_1, part_2, part_3, feat_ref, slope_ref, act, parts,
):
    in_order(near_ref, (act_0, act_1, act_2, act_3), act)
    act_t = act[...].T
    for n, we in enumerate((we_own, we_other)):
        lanes = slice(n * TILE, (n + 1) * TILE)
        bias, theta, live = row_ref[0:1, lanes], row_ref[1:2, lanes], row_ref[2:3, lanes]
        pre = dot(act_t, we[...], ((1,), (0,))) + bias
        gate = jax.nn.sigmoid(SHARPNESS * (pre - theta))
        feat_ref[:, lanes] = (live * pre * gate).astype(BF16)
        slope_ref[lanes, :] = (live * (gate + SHARPNESS * pre * gate * (1.0 - gate))).T
    step = 9 * TILE
    for at in range(0, act.shape[0], step):
        span = slice(at, at + step)
        total = dot(feat_ref[:, :TILE], wd_own[:, span], ((1,), (0,)))
        total = total + dot(feat_ref[:, TILE:], wd_other[:, span], ((1,), (0,)))
        parts[span, :] = total.astype(BF16).T
    cols = part_0.shape[1]
    for n, far, row in chip_rows(near_ref, cols):
        (part_0, part_1, part_2, part_3)[n][far] = parts[pl.ds(row, cols), :]


def decoder_kernel(
    near_ref, res_0, res_1, res_2, res_3, feat_ref, own_ref, other_ref, res, bias
):
    in_order(near_ref, (res_0, res_1, res_2, res_3), res)
    d = res.shape[0]
    quarter, lat = d // NX, TILE // NX
    feat_t = jnp.concatenate([feat_ref[...].T, jnp.ones((16, TILE), BF16)], axis=0)
    bias[...] = jnp.zeros_like(bias)
    for i in range(d // TILE):
        tile = dot(feat_t, res[i * TILE : (i + 1) * TILE, :], ((1,), (1,)))
        bias[i : i + 1, :] = tile[2 * TILE : 2 * TILE + 1, :]
        tile = tile.astype(BF16)
        rows = slice(i * lat, (i + 1) * lat)
        for x in range(NX):
            own_ref[x, rows, :] = tile[x * lat : (x + 1) * lat, :]
            other_ref[x, rows, :] = tile[TILE + x * lat : TILE + (x + 1) * lat, :]
    rows = bias[...].astype(BF16)
    for x in range(NX):
        own_ref[x, quarter:, :] = rows
        other_ref[x, quarter:, :] = rows


def encoder_kernel(
    near_ref, res_0, res_1, res_2, res_3, act_0, act_1, act_2, act_3, wd_own, wd_other, slope_ref,
    own_ref, other_ref, act, res,
):
    in_order(near_ref, (act_0, act_1, act_2, act_3), act)
    in_order(near_ref, (res_0, res_1, res_2, res_3), res)
    quarter = act.shape[0] // NX
    for n, (wd, out) in enumerate(((wd_own, own_ref), (wd_other, other_ref))):
        dfeat = dot(wd[...], res[...], ((1,), (0,)))
        dpre = (dfeat * slope_ref[n * TILE : (n + 1) * TILE, :]).T
        row = jnp.sum(dpre, axis=0, keepdims=True)
        rows = jnp.broadcast_to(row, (ENC_BIAS_ROWS, TILE)).astype(BF16)
        dpre = dpre.astype(BF16)
        for x in range(NX):
            enc = dot(act[x * quarter : (x + 1) * quarter, :], dpre, ((1,), (0,)))
            out[x, :quarter, :] = enc.astype(BF16)
            out[x, quarter:, :] = rows


def place_dec_kernel(parts_ref, dec_ref):
    lat = dec_ref.shape[0] // NX
    for x in range(NX):
        for i in range(dec_ref.shape[1] // TILE):
            rows, lanes = slice(i * lat, (i + 1) * lat), slice(i * TILE, (i + 1) * TILE)
            dec_ref[x * lat : (x + 1) * lat, lanes] = parts_ref[x, rows, :]


def place_enc_kernel(order_ref, *refs):
    enc_ref = refs[-1]
    quarter = enc_ref.shape[0] // NX
    for n, ref in enumerate(refs[:-1]):
        row = pl.multiple_of(order_ref[n] * quarter, quarter)
        enc_ref[pl.ds(row, quarter), :] = ref[:quarter, :]


def call(kernel, outs, args, scratch=(), flops=0):
    whole = pl.BlockSpec(memory_space=pltpu.VMEM)
    scalars = pl.BlockSpec(memory_space=pltpu.SMEM)
    moved = sum(a.size * a.dtype.itemsize for a in args)
    moved += sum(math.prod(s.shape) * s.dtype.itemsize for s in outs)
    return pl.pallas_call(
        kernel,
        out_shape=outs,
        in_specs=[scalars if a.dtype == jnp.int32 else whole for a in args],
        out_specs=[whole] * len(outs),
        scratch_shapes=list(scratch),
        compiler_params=pltpu.CompilerParams(vmem_limit_bytes=VMEM),
        cost_estimate=pl.CostEstimate(flops=0, bytes_accessed=0, transcendentals=0),
    )(*args)


def shape(dims, dtype=BF16):
    return jax.ShapeDtypeStruct(dims, dtype)


def after(value, *others):
    return lax.optimization_barrier((value, *others))[0]


def gather_x(piece):
    behind = lax.ppermute(piece, ALL, AHEAD)
    ahead = lax.ppermute(piece, ALL, BACK)
    return piece, behind, ahead, lax.ppermute(behind, ALL, AHEAD)


def quarter_of(parts, n):
    return [lax.dynamic_index_in_dim(part, n, keepdims=False) for part in parts]


def reduce_gradients(dec, make_enc, core, x):
    ahead, back = (x + 1 + 2 * core) % NX, (x + 3 + 2 * core) % NX
    dec_total = add(dec[0], lax.ppermute(dec[1], "dict", CORE_SWAP))
    enc = make_enc(dec[0])
    dec_moved = lax.all_to_all(dec_total, "dp", 0, 0, axis_index_groups=X_GROUPS)

    enc = enc[0], lax.ppermute(after(enc[1], dec_total), "dict", CORE_SWAP)
    relayed = lax.ppermute(add(*quarter_of(enc, (x + 2) % NX)), ALL, AHEAD)
    direct = lax.ppermute(add(*quarter_of(enc, back)), ALL, BACK)
    onward = add(*quarter_of(enc, ahead), relayed)
    passed = lax.ppermute(onward, ALL, AHEAD)
    dec_moved = after(dec_moved, onward)
    dec_piece = lax.optimization_barrier(add(*[dec_moved[n] for n in range(NX)]))
    enc_piece = lax.optimization_barrier(add(*quarter_of(enc, x), direct, passed))

    dec_sum = add(dec_piece, lax.ppermute(dec_piece, "dp", Y_SWAP))
    enc_sum = add(enc_piece, lax.ppermute(enc_piece, "dp", Y_SWAP))
    copies = jnp.broadcast_to(dec_sum[None], (NX,) + dec_sum.shape)
    dec_whole = lax.all_to_all(copies, "dp", 0, 0, axis_index_groups=X_GROUPS)
    order = jnp.stack([x, back, ahead, (x + 2) % NX]).astype(jnp.int32)
    return dec_sum, dec_whole, gather_x(enc_sum), order


def local(activations, enc_weight, enc_bias, dec_weight, dec_bias, thresholds, active_blocks):
    n_dp = lax.axis_size("dp")
    d = enc_weight.shape[0]
    scale_root = math.sqrt(activations.shape[0] * n_dp)
    dict_index = lax.axis_index("dict")
    core = dict_index % 2

    turned = activations.T
    halves = jnp.stack([turned[:, :TILE], turned[:, TILE:]])
    far = size_of(FAR)
    halves = jnp.broadcast_to(halves[None], (far,) + halves.shape).reshape((-1,) + halves.shape[1:])
    act = exchange(halves, FAR + CORE).reshape(far, -1, TILE)
    chip = dict_index // 2
    own = lax.dynamic_index_in_dim(act, chip // 16 * 4 + chip % 8 // 2, keepdims=False)
    cols = own.shape[0]
    near = chip // 8 % 2 * 2 + chip % 2
    toward = 2 - core
    nears = jnp.stack([near, near ^ toward, near ^ (3 - toward), near ^ 3]).astype(jnp.int32)

    enc_other = lax.ppermute(after(enc_weight, halves), "dict", CORE_SWAP)
    dec_other = lax.ppermute(after(dec_weight, halves), "dict", CORE_SWAP)
    rows = jnp.stack([enc_bias.astype(F32), thresholds.astype(F32) / 16.0])
    rows = jnp.concatenate([rows, lax.ppermute(rows, "dict", CORE_SWAP)], axis=1)
    listed = lax.dynamic_slice_in_dim(active_blocks, core, 1)
    live = jnp.stack([jnp.any(listed == dict_index), jnp.any(listed == (dict_index ^ 1))])
    live = jnp.repeat(live.astype(F32), TILE)[None, :]
    rows = jnp.concatenate([rows, live, jnp.zeros((5, 2 * TILE), F32)], axis=0)

    act, rows = lax.optimization_barrier((act, rows))
    act = gather_near(act)

    work = 2 * d * 2 * TILE * TILE
    *parts, feat, slope = call(
        forward_kernel,
        [
            *[shape(act[0].shape)] * 4,
            shape((TILE, 2 * TILE)),
            shape((2 * TILE, TILE), F32),
        ],
        (nears, *act, enc_weight, enc_other, dec_weight, dec_other, rows),
        [pltpu.VMEM((d, TILE), BF16)] * 2,
        2 * work,
    )

    recon = jnp.sum(exchange(scatter_near(*parts), FAR).astype(F32), axis=0)
    bias = lax.dynamic_slice_in_dim(dec_bias, dict_index // 2 * cols, cols).astype(F32)
    residual = (recon + bias[:, None] - own.astype(F32)) / scale_root
    res = gather_near(spread(residual.astype(BF16), FAR))

    quarter = d // NX
    packed = shape((NX, quarter + DEC_BIAS_ROWS, TILE))
    room = pltpu.VMEM((d, TILE), BF16)
    dec_parts = call(
        decoder_kernel,
        [packed, packed],
        (nears, *res, feat),
        [room, pltpu.VMEM((DEC_BIAS_ROWS, TILE), F32)],
        work,
    )
    packed_enc = shape((NX, quarter + ENC_BIAS_ROWS, TILE))

    def make_enc(*first):
        return call(
            encoder_kernel,
            [packed_enc, packed_enc],
            (nears, *after(res, *first), *act, dec_weight, dec_other, slope),
            [room, room],
            2 * work,
        )

    x = lax.axis_index("dp") // 2
    dec_sum, dec_whole, enc_pieces, order = reduce_gradients(dec_parts, make_enc, core, x)
    (dec,) = call(place_dec_kernel, [shape((TILE, d))], (dec_whole,))
    (enc,) = call(place_enc_kernel, [shape((d, TILE))], (order, *enc_pieces))
    dec_bias_sum = dec_sum[quarter : quarter + d // TILE].reshape(-1)
    return enc, dec, enc_pieces[0][quarter], dec_bias_sum


def solution(mesh):
    placed = (
        P("dp", "dict"),
        P(None, "dict"),
        P("dict"),
        P("dict", None),
        P(),
        P("dict"),
        P("dp", None),
    )
    return jax.shard_map(
        local,
        mesh=mesh,
        in_specs=placed,
        out_specs=(P(None, "dict"), P("dict", None), P("dict"), P()),
        check_vma=False,
    )
```

```python
import math

import jax
import jax.numpy as jnp
import numpy as np
from jax import lax
from jax.experimental import pallas as pl
from jax.experimental.pallas import tpu as pltpu
from jax.sharding import PartitionSpec as P

TILE = 128
SHARPNESS = 4.0
F32 = jnp.float32
BF16 = jnp.bfloat16

GRID = (2, 2, 4, 2, 2)
FAR, NEAR, CORE = (0, 2), (1, 3), (4,)
CHIPS = 32
NX = 4
DEC_BIAS_ROWS, ENC_BIAS_ROWS = 48, 16
VMEM = 48 * 1024 * 1024


def size_of(axes):
    return math.prod(GRID[axis] for axis in axes)


def groups(axes):
    index = np.arange(math.prod(GRID)).reshape(GRID)
    rest = [axis for axis in range(len(GRID)) if axis not in axes]
    return index.transpose(rest + list(axes)).reshape(-1, size_of(axes)).tolist()


ALL = ("dict", "dp")


def along_x(sign):
    pairs = []
    for d in range(64):
        step = sign * (1 - 2 * (d % 2))
        for x in range(NX):
            pairs += [(d * 8 + x * 2 + h, d * 8 + (x + step) % NX * 2 + h) for h in range(2)]
    return pairs


AHEAD, BACK = along_x(1), along_x(-1)
CORE_SWAP = [(i, i ^ 1) for i in range(64)]
Y_SWAP = [(i, i ^ 1) for i in range(8)]


def exchange(parts, axes):
    return lax.all_to_all(parts, "dict", 0, 0, axis_index_groups=groups(axes))


def spread(block, axes):
    return exchange(jnp.broadcast_to(block[None], (size_of(axes),) + block.shape), axes)


def chip_blocks():
    for near in range(4):
        for far in range(8):
            y, z = (far // 4) * 2 + near // 2, (far % 4) * 2 + near % 2
            yield near, far, y * 8 + z


def in_order(parts_ref, whole_ref):
    cols = parts_ref.shape[2]
    for near, far, chip in chip_blocks():
        whole_ref[chip * cols : (chip + 1) * cols, :] = parts_ref[near, far]


def dot(a, b, dims):
    return lax.dot_general(a, b, (dims, ((), ())), preferred_element_type=F32)


def load(refs, rooms, sems):
    copies = [
        pltpu.make_async_copy(ref, room, sems.at[n]) for n, (ref, room) in enumerate(zip(refs, rooms))
    ]
    for copy in copies:
        copy.start()
    return copies


def forward_kernel(
    act_ref, we_own, we_other, wd_own, wd_other, row_ref, parts_ref, feat_ref, slope_ref, act,
    we_0, we_1, wd_0, wd_1, sems,
):
    loads = load((we_own, we_other, wd_own, wd_other), (we_0, we_1, wd_0, wd_1), sems)
    in_order(act_ref, act)
    act_t = act[...].T
    for n, we in enumerate((we_0, we_1)):
        loads[n].wait()
        lanes = slice(n * TILE, (n + 1) * TILE)
        bias, theta, live = row_ref[0:1, lanes], row_ref[1:2, lanes], row_ref[2:3, lanes]
        pre = dot(act_t, we[...], ((1,), (0,))) + bias
        gate = jax.nn.sigmoid(SHARPNESS * (pre - theta))
        feat_ref[:, lanes] = (live * pre * gate).astype(BF16)
        slope_ref[lanes, :] = (live * (gate + SHARPNESS * pre * gate * (1.0 - gate))).T
    cols = parts_ref.shape[2]
    step = 8 * cols
    place = {chip: (near, far) for near, far, chip in chip_blocks()}
    loads[2].wait()
    loads[3].wait()
    for first in range(0, act.shape[0], step):
        span = slice(first, first + step)
        total = dot(feat_ref[:, :TILE], wd_0[:, span], ((1,), (0,)))
        total = total + dot(feat_ref[:, TILE:], wd_1[:, span], ((1,), (0,)))
        turned = total.astype(BF16).T
        for i in range(8):
            near, far = place[first // cols + i]
            parts_ref[near, far] = turned[i * cols : (i + 1) * cols, :]


def decoder_kernel(res_ref, feat_ref, own_ref, other_ref, res, bias):
    in_order(res_ref, res)
    d = res.shape[0]
    quarter, lat = d // NX, TILE // NX
    feat_t = jnp.concatenate([feat_ref[...].T, jnp.ones((16, TILE), BF16)], axis=0)
    bias[...] = jnp.zeros_like(bias)
    for i in range(d // TILE):
        tile = dot(feat_t, res[i * TILE : (i + 1) * TILE, :], ((1,), (1,)))
        bias[i : i + 1, :] = tile[2 * TILE : 2 * TILE + 1, :]
        tile = tile.astype(BF16)
        rows = slice(i * lat, (i + 1) * lat)
        for x in range(NX):
            own_ref[x, rows, :] = tile[x * lat : (x + 1) * lat, :]
            other_ref[x, rows, :] = tile[TILE + x * lat : TILE + (x + 1) * lat, :]
    rows = bias[...].astype(BF16)
    for x in range(NX):
        own_ref[x, quarter:, :] = rows
        other_ref[x, quarter:, :] = rows


def encoder_kernel(
    res_ref, act_ref, wd_own, wd_other, slope_ref, own_ref, other_ref, act, res, wd_0, wd_1, sems
):
    loads = load((wd_own, wd_other), (wd_0, wd_1), sems)
    in_order(act_ref, act)
    in_order(res_ref, res)
    quarter = act.shape[0] // NX
    for n, (wd, out) in enumerate(((wd_0, own_ref), (wd_1, other_ref))):
        loads[n].wait()
        dfeat = dot(wd[...], res[...], ((1,), (0,)))
        dpre = (dfeat * slope_ref[n * TILE : (n + 1) * TILE, :]).T
        row = jnp.sum(dpre, axis=0, keepdims=True)
        rows = jnp.broadcast_to(row, (ENC_BIAS_ROWS, TILE)).astype(BF16)
        dpre = dpre.astype(BF16)
        for x in range(NX):
            enc = dot(act[x * quarter : (x + 1) * quarter, :], dpre, ((1,), (0,)))
            out[x, :quarter, :] = enc.astype(BF16)
            out[x, quarter:, :] = rows


def place_dec_kernel(order_ref, *refs):
    dec_ref = refs[-1]
    lat = dec_ref.shape[0] // NX
    for n, ref in enumerate(refs[:-1]):
        row = pl.multiple_of(order_ref[n] * lat, lat)
        for i in range(dec_ref.shape[1] // TILE):
            lanes = slice(i * TILE, (i + 1) * TILE)
            dec_ref[pl.ds(row, lat), lanes] = ref[i * lat : (i + 1) * lat, :]


def place_enc_kernel(order_ref, *refs):
    enc_ref = refs[-1]
    quarter = enc_ref.shape[0] // NX
    for n, ref in enumerate(refs[:-1]):
        row = pl.multiple_of(order_ref[n] * quarter, quarter)
        enc_ref[pl.ds(row, quarter), :] = ref[:quarter, :]


def call(kernel, outs, args, scratch=(), flops=0, unloaded=()):
    whole = pl.BlockSpec(memory_space=pltpu.VMEM)
    scalars = pl.BlockSpec(memory_space=pltpu.SMEM)
    left = pl.BlockSpec(memory_space=pl.ANY)
    moved = sum(a.size * a.dtype.itemsize for a in args)
    moved += sum(math.prod(s.shape) * s.dtype.itemsize for s in outs)
    return pl.pallas_call(
        kernel,
        out_shape=outs,
        in_specs=[
            scalars if a.dtype == jnp.int32 else left if n in unloaded else whole
            for n, a in enumerate(args)
        ],
        out_specs=[whole] * len(outs),
        scratch_shapes=list(scratch),
        compiler_params=pltpu.CompilerParams(vmem_limit_bytes=VMEM),
        cost_estimate=pl.CostEstimate(flops=flops, bytes_accessed=moved, transcendentals=0),
    )(*args)


def shape(dims, dtype=BF16):
    return jax.ShapeDtypeStruct(dims, dtype)


def add(*terms):
    return sum(term.astype(F32) for term in terms).astype(BF16)


def scatter_x(own, other, ahead, back, x):
    def quarter(n):
        return [lax.dynamic_index_in_dim(part, n, keepdims=False) for part in (own, other)]

    relayed = lax.ppermute(add(*quarter((x + 2) % NX)), ALL, AHEAD)
    direct = lax.ppermute(add(*quarter(back)), ALL, BACK)
    passed = lax.ppermute(add(*quarter(ahead), relayed), ALL, AHEAD)
    return lax.optimization_barrier(add(*quarter(x), direct, passed))


def gather_x(piece):
    behind = lax.ppermute(piece, ALL, AHEAD)
    ahead = lax.ppermute(piece, ALL, BACK)
    return piece, behind, ahead, lax.ppermute(behind, ALL, AHEAD)


def local(activations, enc_weight, enc_bias, dec_weight, dec_bias, thresholds, active_blocks):
    n_dp = lax.axis_size("dp")
    d = enc_weight.shape[0]
    scale_root = math.sqrt(activations.shape[0] * n_dp)
    dict_index = lax.axis_index("dict")
    core = dict_index % 2

    turned = activations.T
    halves = jnp.stack([turned[:, :TILE], turned[:, TILE:]])
    far = size_of(FAR)
    halves = jnp.broadcast_to(halves[None], (far,) + halves.shape).reshape((-1,) + halves.shape[1:])
    act = exchange(halves, FAR + CORE).reshape(far, -1, TILE)
    chip = dict_index // 2
    own = lax.dynamic_index_in_dim(act, chip // 16 * 4 + chip % 8 // 2, keepdims=False)
    cols = own.shape[0]
    act = spread(act, NEAR)

    enc_other = lax.ppermute(enc_weight, "dict", CORE_SWAP)
    dec_other = lax.ppermute(dec_weight, "dict", CORE_SWAP)
    rows = jnp.stack([enc_bias.astype(F32), thresholds.astype(F32) / 16.0])
    rows = jnp.concatenate([rows, lax.ppermute(rows, "dict", CORE_SWAP)], axis=1)
    listed = lax.dynamic_slice_in_dim(active_blocks, core, 1)
    live = jnp.stack([jnp.any(listed == dict_index), jnp.any(listed == (dict_index ^ 1))])
    live = jnp.repeat(live.astype(F32), TILE)[None, :]
    rows = jnp.concatenate([rows, live, jnp.zeros((5, 2 * TILE), F32)], axis=0)

    work = 2 * d * 2 * TILE * TILE
    parts, feat, slope = call(
        forward_kernel,
        [
            shape(act.shape),
            shape((TILE, 2 * TILE)),
            shape((2 * TILE, TILE), F32),
        ],
        (act, enc_weight, enc_other, dec_weight, dec_other, rows),
        [
            pltpu.VMEM((d, TILE), BF16),
            *[pltpu.VMEM((d, TILE), BF16)] * 2,
            *[pltpu.VMEM((TILE, d), BF16)] * 2,
            pltpu.SemaphoreType.DMA((4,)),
        ],
        2 * work,
        (1, 2, 3, 4),
    )

    near_sum = jnp.sum(exchange(parts, NEAR).astype(F32), axis=0).astype(BF16)
    recon = jnp.sum(exchange(near_sum, FAR).astype(F32), axis=0)
    bias = lax.dynamic_slice_in_dim(dec_bias, dict_index // 2 * cols, cols).astype(F32)
    residual = (recon + bias[:, None] - own.astype(F32)) / scale_root
    res = spread(spread(residual.astype(BF16), FAR), NEAR)

    quarter = d // NX
    packed = shape((NX, quarter + DEC_BIAS_ROWS, TILE))
    room = pltpu.VMEM((d, TILE), BF16)
    dec_parts = call(
        decoder_kernel,
        [packed, packed],
        (res, feat),
        [room, pltpu.VMEM((DEC_BIAS_ROWS, TILE), F32)],
        work,
    )
    dec_parts, res = lax.optimization_barrier((dec_parts, res))
    packed = shape((NX, quarter + ENC_BIAS_ROWS, TILE))
    enc_parts = call(
        encoder_kernel,
        [packed, packed],
        (res, act, dec_weight, dec_other, slope),
        [room, room, *[pltpu.VMEM((TILE, d), BF16)] * 2, pltpu.SemaphoreType.DMA((2,))],
        2 * work,
        (2, 3),
    )

    x = lax.axis_index("dp") // 2
    ahead, back = (x + 1 + 2 * core) % NX, (x + 3 + 2 * core) % NX
    order = jnp.stack([x, back, ahead, (x + 2) % NX]).astype(jnp.int32)
    dec_other = lax.ppermute(dec_parts[1], "dict", CORE_SWAP)
    enc_other, dec_other = lax.optimization_barrier((enc_parts[1], dec_other))
    enc_other = lax.ppermute(enc_other, "dict", CORE_SWAP)
    dec_piece = scatter_x(dec_parts[0], dec_other, ahead, back, x)
    enc_piece = scatter_x(enc_parts[0], enc_other, ahead, back, x)
    dec_piece = add(dec_piece, lax.ppermute(dec_piece, "dp", Y_SWAP))
    enc_piece = add(enc_piece, lax.ppermute(enc_piece, "dp", Y_SWAP))
    (dec,) = call(place_dec_kernel, [shape((TILE, d))], (order, *gather_x(dec_piece)))
    (enc,) = call(place_enc_kernel, [shape((d, TILE))], (order, *gather_x(enc_piece)))
    return enc, dec, enc_piece[quarter], dec_piece[quarter : quarter + d // TILE].reshape(-1)


def solution(mesh):
    placed = (
        P("dp", "dict"),
        P(None, "dict"),
        P("dict"),
        P("dict", None),
        P(),
        P("dict"),
        P("dp", None),
    )
    return jax.shard_map(
        local,
        mesh=mesh,
        in_specs=placed,
        out_specs=(P(None, "dict"), P("dict", None), P("dict"), P()),
        check_vma=False,
    )
```

```python
import math

import jax
import jax.numpy as jnp
import numpy as np
from jax import lax
from jax.experimental import pallas as pl
from jax.experimental.pallas import tpu as pltpu
from jax.sharding import PartitionSpec as P

TILE = 128
SHARPNESS = 4.0
F32 = jnp.float32
BF16 = jnp.bfloat16

GRID = (2, 2, 4, 2, 2)
FAR, NEAR, CORE = (0, 2), (1, 3), (4,)
CHIPS = 32
NX = 4
DEC_BIAS_ROWS, ENC_BIAS_ROWS = 48, 16
VMEM = 48 * 1024 * 1024


def size_of(axes):
    return math.prod(GRID[axis] for axis in axes)


def groups(axes):
    index = np.arange(math.prod(GRID)).reshape(GRID)
    rest = [axis for axis in range(len(GRID)) if axis not in axes]
    return index.transpose(rest + list(axes)).reshape(-1, size_of(axes)).tolist()


ALL = ("dict", "dp")


def along_x(sign):
    pairs = []
    for d in range(64):
        step = sign * (1 - 2 * (d % 2))
        for x in range(NX):
            pairs += [(d * 8 + x * 2 + h, d * 8 + (x + step) % NX * 2 + h) for h in range(2)]
    return pairs


AHEAD, BACK = along_x(1), along_x(-1)
CORE_SWAP = [(i, i ^ 1) for i in range(64)]
Y_SWAP = [(i, i ^ 1) for i in range(8)]


def exchange(parts, axes):
    return lax.all_to_all(parts, "dict", 0, 0, axis_index_groups=groups(axes))


def spread(block, axes):
    return exchange(jnp.broadcast_to(block[None], (size_of(axes),) + block.shape), axes)


def chip_blocks():
    for near in range(4):
        for far in range(8):
            y, z = (far // 4) * 2 + near // 2, (far % 4) * 2 + near % 2
            yield near, far, y * 8 + z


def in_order(parts_ref, whole_ref):
    cols = parts_ref.shape[2]
    for near, far, chip in chip_blocks():
        whole_ref[chip * cols : (chip + 1) * cols, :] = parts_ref[near, far]


def dot(a, b, dims):
    return lax.dot_general(a, b, (dims, ((), ())), preferred_element_type=F32)


def load(refs, rooms, sems):
    copies = [
        pltpu.make_async_copy(ref, room, sems.at[n]) for n, (ref, room) in enumerate(zip(refs, rooms))
    ]
    for copy in copies:
        copy.start()
    return copies


def forward_kernel(
    act_ref, we_own, we_other, wd_own, wd_other, row_ref, parts_ref, feat_ref, slope_ref, act,
    we_0, we_1, wd_0, wd_1, sems,
):
    loads = load((we_own, we_other, wd_own, wd_other), (we_0, we_1, wd_0, wd_1), sems)
    in_order(act_ref, act)
    act_t = act[...].T
    for n, we in enumerate((we_0, we_1)):
        loads[n].wait()
        lanes = slice(n * TILE, (n + 1) * TILE)
        bias, theta, live = row_ref[0:1, lanes], row_ref[1:2, lanes], row_ref[2:3, lanes]
        pre = dot(act_t, we[...], ((1,), (0,))) + bias
        gate = jax.nn.sigmoid(SHARPNESS * (pre - theta))
        feat_ref[:, lanes] = (live * pre * gate).astype(BF16)
        slope_ref[lanes, :] = (live * (gate + SHARPNESS * pre * gate * (1.0 - gate))).T
    cols = parts_ref.shape[2]
    step = 8 * cols
    place = {chip: (near, far) for near, far, chip in chip_blocks()}
    loads[2].wait()
    loads[3].wait()
    for first in range(0, act.shape[0], step):
        span = slice(first, first + step)
        total = dot(feat_ref[:, :TILE], wd_0[:, span], ((1,), (0,)))
        total = total + dot(feat_ref[:, TILE:], wd_1[:, span], ((1,), (0,)))
        turned = total.astype(BF16).T
        for i in range(8):
            near, far = place[first // cols + i]
            parts_ref[near, far] = turned[i * cols : (i + 1) * cols, :]


def decoder_kernel(res_ref, feat_ref, own_ref, other_ref, res, bias):
    in_order(res_ref, res)
    d = res.shape[0]
    quarter, lat = d // NX, TILE // NX
    feat_t = jnp.concatenate([feat_ref[...].T, jnp.ones((16, TILE), BF16)], axis=0)
    bias[...] = jnp.zeros_like(bias)
    for i in range(d // TILE):
        tile = dot(feat_t, res[i * TILE : (i + 1) * TILE, :], ((1,), (1,)))
        bias[i : i + 1, :] = tile[2 * TILE : 2 * TILE + 1, :]
        tile = tile.astype(BF16)
        rows = slice(i * lat, (i + 1) * lat)
        for x in range(NX):
            own_ref[x, rows, :] = tile[x * lat : (x + 1) * lat, :]
            other_ref[x, rows, :] = tile[TILE + x * lat : TILE + (x + 1) * lat, :]
    rows = bias[...].astype(BF16)
    for x in range(NX):
        own_ref[x, quarter:, :] = rows
        other_ref[x, quarter:, :] = rows


def encoder_kernel(
    res_ref, act_ref, wd_own, wd_other, slope_ref, own_ref, other_ref, act, res, wd_0, wd_1, sems
):
    loads = load((wd_own, wd_other), (wd_0, wd_1), sems)
    in_order(act_ref, act)
    in_order(res_ref, res)
    quarter = act.shape[0] // NX
    for n, (wd, out) in enumerate(((wd_0, own_ref), (wd_1, other_ref))):
        loads[n].wait()
        dfeat = dot(wd[...], res[...], ((1,), (0,)))
        dpre = (dfeat * slope_ref[n * TILE : (n + 1) * TILE, :]).T
        row = jnp.sum(dpre, axis=0, keepdims=True)
        rows = jnp.broadcast_to(row, (ENC_BIAS_ROWS, TILE)).astype(BF16)
        dpre = dpre.astype(BF16)
        for x in range(NX):
            enc = dot(act[x * quarter : (x + 1) * quarter, :], dpre, ((1,), (0,)))
            out[x, :quarter, :] = enc.astype(BF16)
            out[x, quarter:, :] = rows


def place_dec_kernel(order_ref, *refs):
    dec_ref = refs[-1]
    lat = dec_ref.shape[0] // NX
    for n, ref in enumerate(refs[:-1]):
        row = pl.multiple_of(order_ref[n] * lat, lat)
        for i in range(dec_ref.shape[1] // TILE):
            lanes = slice(i * TILE, (i + 1) * TILE)
            dec_ref[pl.ds(row, lat), lanes] = ref[i * lat : (i + 1) * lat, :]


def place_enc_kernel(order_ref, *refs):
    *pieces, enc_ref, sems = refs
    quarter = enc_ref.shape[0] // NX
    copies = []
    for n, ref in enumerate(pieces):
        row = pl.multiple_of(order_ref[n] * quarter, quarter)
        rows = enc_ref.at[pl.ds(row, quarter), :]
        copies.append(pltpu.make_async_copy(ref.at[pl.ds(0, quarter), :], rows, sems.at[n]))
        copies[-1].start()
    for copy in copies:
        copy.wait()


def call(kernel, outs, args, scratch=(), flops=0, unloaded=(), in_place=False):
    whole = pl.BlockSpec(memory_space=pltpu.VMEM)
    scalars = pl.BlockSpec(memory_space=pltpu.SMEM)
    left = pl.BlockSpec(memory_space=pl.ANY)
    moved = sum(a.size * a.dtype.itemsize for a in args)
    moved += sum(math.prod(s.shape) * s.dtype.itemsize for s in outs)
    return pl.pallas_call(
        kernel,
        out_shape=outs,
        in_specs=[
            scalars if a.dtype == jnp.int32 else left if n in unloaded else whole
            for n, a in enumerate(args)
        ],
        out_specs=[left if in_place else whole] * len(outs),
        scratch_shapes=list(scratch),
        compiler_params=pltpu.CompilerParams(vmem_limit_bytes=VMEM),
        cost_estimate=pl.CostEstimate(flops=flops, bytes_accessed=moved, transcendentals=0),
    )(*args)


def shape(dims, dtype=BF16):
    return jax.ShapeDtypeStruct(dims, dtype)


def add(*terms):
    return sum(term.astype(F32) for term in terms).astype(BF16)


def scatter_x(own, other, ahead, back, x):
    def quarter(n):
        return [lax.dynamic_index_in_dim(part, n, keepdims=False) for part in (own, other)]

    relayed = lax.ppermute(add(*quarter((x + 2) % NX)), ALL, AHEAD)
    direct = lax.ppermute(add(*quarter(back)), ALL, BACK)
    passed = lax.ppermute(add(*quarter(ahead), relayed), ALL, AHEAD)
    return lax.optimization_barrier(add(*quarter(x), direct, passed))


def gather_x(piece):
    behind = lax.ppermute(piece, ALL, AHEAD)
    ahead = lax.ppermute(piece, ALL, BACK)
    return piece, behind, ahead, lax.ppermute(behind, ALL, AHEAD)


def local(activations, enc_weight, enc_bias, dec_weight, dec_bias, thresholds, active_blocks):
    n_dp = lax.axis_size("dp")
    d = enc_weight.shape[0]
    scale_root = math.sqrt(activations.shape[0] * n_dp)
    dict_index = lax.axis_index("dict")
    core = dict_index % 2

    turned = activations.T
    halves = jnp.stack([turned[:, :TILE], turned[:, TILE:]])
    far = size_of(FAR)
    halves = jnp.broadcast_to(halves[None], (far,) + halves.shape).reshape((-1,) + halves.shape[1:])
    act = exchange(halves, FAR + CORE).reshape(far, -1, TILE)
    chip = dict_index // 2
    own = lax.dynamic_index_in_dim(act, chip // 16 * 4 + chip % 8 // 2, keepdims=False)
    cols = own.shape[0]
    act = spread(act, NEAR)

    enc_other = lax.ppermute(enc_weight, "dict", CORE_SWAP)
    dec_other = lax.ppermute(dec_weight, "dict", CORE_SWAP)
    rows = jnp.stack([enc_bias.astype(F32), thresholds.astype(F32) / 16.0])
    rows = jnp.concatenate([rows, lax.ppermute(rows, "dict", CORE_SWAP)], axis=1)
    listed = lax.dynamic_slice_in_dim(active_blocks, core, 1)
    live = jnp.stack([jnp.any(listed == dict_index), jnp.any(listed == (dict_index ^ 1))])
    live = jnp.repeat(live.astype(F32), TILE)[None, :]
    rows = jnp.concatenate([rows, live, jnp.zeros((5, 2 * TILE), F32)], axis=0)

    work = 2 * d * 2 * TILE * TILE
    parts, feat, slope = call(
        forward_kernel,
        [
            shape(act.shape),
            shape((TILE, 2 * TILE)),
            shape((2 * TILE, TILE), F32),
        ],
        (act, enc_weight, enc_other, dec_weight, dec_other, rows),
        [
            pltpu.VMEM((d, TILE), BF16),
            *[pltpu.VMEM((d, TILE), BF16)] * 2,
            *[pltpu.VMEM((TILE, d), BF16)] * 2,
            pltpu.SemaphoreType.DMA((4,)),
        ],
        2 * work,
        (1, 2, 3, 4),
    )

    near_sum = jnp.sum(exchange(parts, NEAR).astype(F32), axis=0).astype(BF16)
    recon = jnp.sum(exchange(near_sum, FAR).astype(F32), axis=0)
    bias = lax.dynamic_slice_in_dim(dec_bias, dict_index // 2 * cols, cols).astype(F32)
    residual = (recon + bias[:, None] - own.astype(F32)) / scale_root
    res = spread(spread(residual.astype(BF16), FAR), NEAR)

    quarter = d // NX
    packed = shape((NX, quarter + DEC_BIAS_ROWS, TILE))
    room = pltpu.VMEM((d, TILE), BF16)
    dec_parts = call(
        decoder_kernel,
        [packed, packed],
        (res, feat),
        [room, pltpu.VMEM((DEC_BIAS_ROWS, TILE), F32)],
        work,
    )
    dec_parts, res = lax.optimization_barrier((dec_parts, res))
    packed = shape((NX, quarter + ENC_BIAS_ROWS, TILE))
    enc_parts = call(
        encoder_kernel,
        [packed, packed],
        (res, act, dec_weight, dec_other, slope),
        [room, room, *[pltpu.VMEM((TILE, d), BF16)] * 2, pltpu.SemaphoreType.DMA((2,))],
        2 * work,
        (2, 3),
    )

    x = lax.axis_index("dp") // 2
    ahead, back = (x + 1 + 2 * core) % NX, (x + 3 + 2 * core) % NX
    order = jnp.stack([x, back, ahead, (x + 2) % NX]).astype(jnp.int32)
    dec_other = lax.ppermute(dec_parts[1], "dict", CORE_SWAP)
    enc_other, dec_other = lax.optimization_barrier((enc_parts[1], dec_other))
    enc_other = lax.ppermute(enc_other, "dict", CORE_SWAP)
    dec_piece = scatter_x(dec_parts[0], dec_other, ahead, back, x)
    enc_piece = scatter_x(enc_parts[0], enc_other, ahead, back, x)
    dec_piece = add(dec_piece, lax.ppermute(dec_piece, "dp", Y_SWAP))
    enc_piece = add(enc_piece, lax.ppermute(enc_piece, "dp", Y_SWAP))
    (dec,) = call(place_dec_kernel, [shape((TILE, d))], (order, *gather_x(dec_piece)))
    (enc,) = call(
        place_enc_kernel,
        [shape((d, TILE))],
        (order, *gather_x(enc_piece)),
        [pltpu.SemaphoreType.DMA((NX,))],
        unloaded=(1, 2, 3, 4),
        in_place=True,
    )
    return enc, dec, enc_piece[quarter], dec_piece[quarter : quarter + d // TILE].reshape(-1)


def solution(mesh):
    placed = (
        P("dp", "dict"),
        P(None, "dict"),
        P("dict"),
        P("dict", None),
        P(),
        P("dict"),
        P("dp", None),
    )
    return jax.shard_map(
        local,
        mesh=mesh,
        in_specs=placed,
        out_specs=(P(None, "dict"), P("dict", None), P("dict"), P()),
        check_vma=False,
    )
```
